512 devices in a mesh: dp: 64 (over z, x), expert: 8 (over y, core).
Axes of the slice: x: 4, y: 4, z: 16, core: 2. Of those that a mesh axis runs over, the one named last changes fastest.
Arguments:
- stream_grad: bfloat16 [65536, 4096], P('dp', 'expert'), may hold values from -6 to 6
- value_grad: bfloat16 [65536, 1024], P(('dp', 'expert')), may hold values from -24 to 24
- attn_input: bfloat16 [65536, 4096], P('dp', 'expert'), may hold values from -200 to 200
- norm_gain: float32 [4096], P('expert'), may hold values from 0.1 to 1.9
- value_weight: bfloat16 [1024, 4096], P('dp', 'expert'), may hold values from -0.1875 to 0.1875
- gate_logits: float32 [65536, 2], P('dp'), may hold values from -6 to 6
- routes: int32 [65536, 2], P('dp'), may hold values from 0 to 7, all different within a row; in each aligned block of 1024 rows (0 to 1023, 1024 to 2047, ...) at most 320 rows name the same one
Outputs:
- d_value: bfloat16 [1024, 4096], P('dp', 'expert')
- d_gain: float32 [4096], P('expert')
- dispatched: bfloat16 [8, 20480, 4096], P('expert', 'dp')
The draws below stay inside these ranges and needn't reach their ends.
Inputs may be any that keep to these rules, and one draw needn't show every extreme that they name: `routes`: among the rows of one block of 1024 tokens no expert is named by more than 320 rows, and in some blocks one expert is named by exactly 320 rows; the two experts of a token differ.
All inputs are finite; a program needn't handle non-finite values.
Results may differ from the reference program's by a relative error of at most 0.005.
Values may be sent and summed in bfloat16 or wider, within the bound.
No kernel may reach another device: no remote copies, remote signals or barrier semaphores. Data moves between devices by JAX's collectives and lax.ppermute only.
A program may use at most 64 MiB of HBM per device.

```python
import math
import jax
import jax.numpy as jnp
import numpy as np
from jax import lax

D = 4096
KV = 1024
EXPERTS = 8
GROUP = 1024
CAP = 320
TOKENS = 65536


def draw_attn_input(key, part):
    key = jax.random.fold_in(key, 11)
    row_key, col_key, base_key = jax.random.split(key, 3)
    row_ramp = 1.0 + 2.0 * jnp.arange(TOKENS, dtype=jnp.float32)[:, None] / TOKENS
    col_ramp = 1.0 + 2.0 * jnp.arange(D, dtype=jnp.float32)[None, :] / D
    row_scale = jnp.exp(jax.random.uniform(row_key, (TOKENS, 1), jnp.float32, math.log(0.05), math.log(0.5))) * row_ramp
    col_scale = jnp.exp(jax.random.uniform(col_key, (1, D), jnp.float32, 0.0, math.log(10.0))) * col_ramp
    base = jnp.clip(jax.random.normal(base_key, (TOKENS, D), jnp.float32), -4.0, 4.0)
    return (base * row_scale * col_scale).astype(jnp.bfloat16)


def strengthened(entries, key, source, target, parts, factor):
    def block_of(axis_at):
        return (jnp.arange(entries.shape[axis_at]) // (entries.shape[axis_at] // parts)).reshape((-1,) + (1,) * (entries.ndim - 1 - axis_at))

    one_side = jax.random.permutation(key, parts)[block_of(target)]
    other_side = (block_of(target) + parts // 2) % parts
    return jnp.where((block_of(source) == one_side) | (block_of(source) == other_side), factor * entries, entries)


def block_levels(key, extent, shards, smallest, top_value):
    factor_of, own = 1.0, jax.random.fold_in(key, 6)
    for position, shards_of in shards:
        heights = jnp.exp(jax.random.uniform(jax.random.fold_in(own, position), (shards_of,), jnp.float32, smallest / len(shards), top_value / len(shards)))
        factor_of = factor_of * jnp.repeat(heights, extent[position] // shards_of).reshape([-1 if axis == position else 1 for axis in range(len(extent))])
    return factor_of


def assign_block(key, own, number, rows, amount, top, bound, skew):
    ranking = jax.random.permutation(key, amount)
    heavy_load, usual = portions_of(amount, rows * top, bound, skew, True), portions_of(amount, rows * top, bound, skew, False)
    places = jnp.arange(amount)

    def named(sizes, offset_by):
        used = int((sizes > 0).sum())
        fixed = max(1, used // 4)
        shifted = fixed + (places - fixed + offset_by * (used - fixed)) % max(1, amount - fixed)
        return jnp.zeros((amount,), jnp.int32).at[ranking[jnp.where(places < fixed, places, shifted)]].set(jnp.asarray(sizes, jnp.int32))

    sizes = jnp.where(number % 4 == 0, named(heavy_load, number // 4), named(usual, number - number // 4 - 1))
    mixed = jax.random.permutation(jax.random.fold_in(own, 3), amount)
    source_of, taker = mixed[0:amount // 2 * 2:2], mixed[1:amount // 2 * 2:2]
    room = jnp.minimum(sizes[source_of] - 1, bound - sizes[taker]) // 2
    room = jnp.where((source_of == ranking[0]) | (taker == ranking[0]) | (sizes[taker] == 0), 0, jnp.maximum(room, 0))
    shifted = jax.random.randint(jax.random.fold_in(own, 4), (amount // 2,), 0, 1 << 20) % (room + 1)
    sizes = sizes.at[source_of].add(-shifted).at[taker].add(shifted)
    items = jnp.searchsorted(jnp.cumsum(sizes), jnp.arange(rows * top), side="right").astype(jnp.int32)
    table = items.reshape(top, rows).T
    table = table[jax.random.permutation(jax.random.fold_in(own, 1), rows)]
    offset_by = jax.random.randint(jax.random.fold_in(own, 2), (rows, 1), 0, top)
    return jnp.take_along_axis(table, (jnp.arange(top)[None, :] + offset_by) % top, axis=1)


def portions_of(number_of, total, reach, slope, full):
    portions = [(1 << 20) // math.isqrt(rank ** slope) + 1 for rank in range(1, number_of + 1)]
    largest = reach if full else min(reach, max(-(-total // number_of), total * portions[0] // sum(portions)))
    least = 1 if total - largest >= number_of - 1 else 0
    counts, surplus = [largest] + [least] * (number_of - 1), total - largest - least * (number_of - 1)
    while surplus > 0:
        movable = [i for i in range(1, number_of) if counts[i] < largest] or [i for i in range(1, number_of) if counts[i] < reach]
        whole, budget = sum([portions[i] for i in movable]), surplus
        for i in movable:
            extra = min(reach - counts[i], max(1, budget * portions[i] // whole), surplus)
            counts[i] = counts[i] + extra
            surplus = surplus - extra
    return np.array(counts)


def normal_values(rng, extent, width, reach, cuts=(), held_as=jnp.bfloat16):
    gain = block_levels(rng, extent, cuts, -0.22, 0.18) if cuts else 1.0
    drawn = jax.random.normal(rng, extent, jnp.float32) * width * gain
    return jnp.minimum(jnp.maximum(drawn, -reach), reach).astype(held_as)


def noise_with(rng, dims, scale, reach, cuts, heavy, kind=jnp.bfloat16):
    result = scale * jax.random.normal(rng, dims, jnp.float32)
    if cuts:
        result = result * block_levels(rng, dims, cuts, -0.22, 0.18)
    return jnp.clip(strengthened(result, jax.random.fold_in(rng, 3), *heavy), -reach, reach).astype(kind)


def setup_inputs(seed: int = 0) -> dict:
    arg_keys = jax.random.split(jax.random.key(seed), 8)
    stream_grad = normal_values(arg_keys[0], (TOKENS, D), 0.5, 6.0, ((0, 64), (1, 8)))
    value_grad = noise_with(arg_keys[1], (TOKENS, KV), 1.0, 24.0, ((0, 512),), (0, 1, 512, 6.0))
    attn_input = draw_attn_input(jax.random.fold_in(arg_keys[7], 71), 0)
    norm_gain = jnp.clip(1.0 + 0.18 * jax.random.normal(arg_keys[3], (D,), jnp.float32), 0.1, 1.9)
    value_weight = normal_values(arg_keys[4], (KV, D), KV ** -0.5, 0.1875, ((0, 64), (1, 8)))
    gate_logits = normal_values(arg_keys[5], (TOKENS, 2), 1.5, 6.0, ((0, 64),), jnp.float32)
    routes_keys = jax.random.split(jax.random.fold_in(arg_keys[6], 1), TOKENS // GROUP)
    routes_turns = jax.random.permutation(jax.random.fold_in(arg_keys[6], 3), TOKENS // GROUP)
    routes = jax.vmap(lambda own, number: assign_block(jax.random.fold_in(arg_keys[6], 2), own, number, GROUP, EXPERTS, 2, CAP, 1))(routes_keys, routes_turns).reshape((TOKENS, 2))
    return {"stream_grad": stream_grad, "value_grad": value_grad, "attn_input": attn_input, "norm_gain": norm_gain, "value_weight": value_weight, "gate_logits": gate_logits, "routes": routes}


epsilon = 1e-05

def reference(stream_grad, value_grad, attn_input, norm_gain, value_weight, gate_logits, routes):
    blocks = TOKENS // GROUP
    rescale = float(TOKENS) ** (-0.5)

    def group_pass(carry, operands):
        value_sum, gain_sum = carry
        grads_in, values_in, inputs_in, logits_in, routes_in = operands
        inputs = inputs_in.astype(jnp.float32)
        root_mean = jnp.sqrt(lax.optimization_barrier(jnp.mean(inputs * inputs, axis=-1, keepdims=True)) + epsilon)
        scaled = inputs / root_mean
        normed = (scaled * norm_gain).astype(jnp.bfloat16)
        value_sum = value_sum + jnp.dot(values_in.T, normed, preferred_element_type=jnp.float32)
        d_normed = jnp.dot(values_in, value_weight, preferred_element_type=jnp.float32)
        gain_sum = gain_sum + lax.optimization_barrier(jnp.sum(d_normed * scaled, axis=0))
        weighted = d_normed * norm_gain
        stream = grads_in.astype(jnp.float32) + (weighted - scaled * lax.optimization_barrier(jnp.mean(weighted * scaled, axis=-1, keepdims=True))) / root_mean
        gate_prob = 1.0 / (1.0 + jnp.exp(logits_in[:, ::-1] - logits_in))
        flat_routes = routes_in.reshape(-1).astype(jnp.int32)
        onehot = (flat_routes[:, None] == jnp.arange(EXPERTS, dtype=jnp.int32)[None, :]).astype(jnp.int32)
        slot_index = lax.optimization_barrier(jnp.sum((jnp.cumsum(onehot, axis=0) - onehot) * onehot, axis=-1)).astype(jnp.int32)
        sent_rows = (gate_prob[:, :, None] * stream[:, None, :]).astype(jnp.bfloat16).reshape(-1, D)
        block = jnp.zeros((EXPERTS, CAP, D), jnp.bfloat16).at[flat_routes, slot_index].set(sent_rows)
        return ((value_sum, gain_sum), block)
    operands = (stream_grad.reshape(blocks, GROUP, D), value_grad.reshape(blocks, GROUP, KV), attn_input.reshape(blocks, GROUP, D), gate_logits.reshape(blocks, GROUP, 2), routes.reshape(blocks, GROUP, 2))
    initial = (jnp.zeros((KV, D), jnp.float32), jnp.zeros((D,), jnp.float32))
    (value_sum, gain_sum), pieces = lax.scan(group_pass, initial, operands)
    d_value = (value_sum * rescale).astype(jnp.bfloat16)
    d_gain = gain_sum * rescale
    dispatched = jnp.transpose(pieces, (1, 0, 2, 3)).reshape(EXPERTS, blocks * CAP, D)
    return (d_value, d_gain, dispatched)
```

```python
import jax
import jax.numpy as jnp
from jax import lax
from jax.experimental import pallas as pl
from jax.experimental.pallas import tpu as pltpu
from jax.sharding import Mesh, PartitionSpec as P

epsilon = 1e-05
EXPERT = ("y", "core")


def route_kernel(routes_ref, logits_ref, slot_ref, gate_ref):
    experts, group = slot_ref.shape
    expert = lax.broadcasted_iota(jnp.int32, (experts, group), 0)
    first = routes_ref[0:1, :] == expert
    second = routes_ref[1:2, :] == expert
    named = jnp.where(first | second, 1.0, 0.0)
    earlier = lax.broadcasted_iota(jnp.int32, (group, group), 0) < lax.broadcasted_iota(
        jnp.int32, (group, group), 1
    )
    count = jnp.dot(
        named.astype(jnp.bfloat16),
        jnp.where(earlier, 1.0, 0.0).astype(jnp.bfloat16),
        preferred_element_type=jnp.float32,
    )
    slot_ref[...] = jnp.where(named > 0.0, count, -1.0).astype(jnp.int32)
    low, high = logits_ref[0:1, :], logits_ref[1:2, :]
    gate_first = 1.0 / (1.0 + jnp.exp(high - low))
    gate_second = 1.0 / (1.0 + jnp.exp(low - high))
    gate_ref[...] = jnp.where(first, gate_first, jnp.where(second, gate_second, 0.0))


def column(row):
    return jnp.transpose(jnp.broadcast_to(row, (8, row.shape[1])))[:, 0:1]


def dispatch_kernel(
    width, squares_ref, inner_ref, gain_ref, slot_ref, gate_ref, grad_ref, input_ref, normed_ref,
    out_ref, stream_ref,
):
    expert = pl.program_id(0)
    group = grad_ref.shape[0]
    capacity = out_ref.shape[1]

    @pl.when(expert == 0)
    def _():
        squares = jnp.sum(squares_ref[...], axis=0, keepdims=True)
        root_mean = jnp.sqrt(squares / width + epsilon)
        inner = jnp.sum(inner_ref[...], axis=0, keepdims=True) / width
        root_column, inner_column = column(root_mean), column(inner)
        scaled = input_ref[...].astype(jnp.float32) / root_column
        weighted = normed_ref[...] * gain_ref[...]
        stream_ref[...] = (
            grad_ref[...].astype(jnp.float32) + (weighted - scaled * inner_column) / root_column
        )

    slot = slot_ref[pl.ds(expert, 1), :]
    gate = column(gate_ref[pl.ds(expert, 1), :])
    rows = (gate * stream_ref[...]).astype(jnp.bfloat16)
    taken = lax.broadcasted_iota(jnp.int32, (capacity, group), 0) == slot
    picked = jnp.dot(
        jnp.where(taken, 1.0, 0.0).astype(jnp.bfloat16), rows, preferred_element_type=jnp.float32
    )
    out_ref[0] = picked.astype(jnp.bfloat16)


def to_all(part, axis):
    size = lax.axis_size(axis)
    return lax.all_to_all(
        jnp.broadcast_to(part[None], (size,) + part.shape), axis, 0, 0, tiled=True
    )


def swapped(parts, axis):
    return lax.all_to_all(parts, axis, 0, 0, tiled=True)


def on_device(stream_grad, value_grad, attn_input, norm_gain, value_weight, gate_logits, routes):
    group, columns = attn_input.shape
    experts = lax.axis_size(EXPERT)
    zh, zl, xs = lax.axis_size("zh"), lax.axis_size("zl"), lax.axis_size("x")
    width = columns * experts
    tokens_all = group * zh * zl * xs
    rescale = float(tokens_all) ** (-0.5)
    capacity = min(group, 5 * group // (2 * experts))
    rows = value_weight.shape[0]
    features = rows * zh * zl * xs
    vmem = pl.BlockSpec(memory_space=pltpu.VMEM)

    every_value = lax.all_gather(value_grad, EXPERT, axis=0, tiled=True)

    weight = to_all(value_weight, "zh")
    weight = to_all(weight, "zl")
    weight = to_all(weight, "x")
    weight = jnp.transpose(weight, (2, 1, 0, 3, 4)).reshape(features, columns)

    slot, gate = pl.pallas_call(
        route_kernel,
        in_specs=[vmem, vmem],
        out_specs=[vmem, vmem],
        out_shape=[
            jax.ShapeDtypeStruct((experts, group), jnp.int32),
            jax.ShapeDtypeStruct((experts, group), jnp.float32),
        ],
        compiler_params=pltpu.CompilerParams(vmem_limit_bytes=32 * 2**20),
    )(routes.T, gate_logits.T)

    inputs = attn_input.astype(jnp.float32)
    own_squares = jnp.sum(inputs * inputs, axis=1)
    squares = to_all(own_squares.reshape(8, group // 8), EXPERT).reshape(experts, group)
    root_mean = jnp.sqrt(jnp.sum(squares, axis=0) / width + epsilon)[:, None]
    scaled = inputs / root_mean
    normed = (scaled * norm_gain).astype(jnp.bfloat16)

    d_value = lax.dot_general(
        every_value, normed, (((0,), (0,)), ((), ())), preferred_element_type=jnp.float32
    )
    d_value = d_value.reshape(zh, zl, xs, rows, columns).transpose(2, 1, 0, 3, 4)
    d_value = swapped(d_value.astype(jnp.bfloat16), "x").astype(jnp.float32).sum(axis=0)

    d_normed = jnp.dot(every_value, weight, preferred_element_type=jnp.float32)
    weighted = d_normed * norm_gain
    own_inner = jnp.sum(weighted * scaled, axis=1)
    inner = to_all(own_inner.reshape(8, group // 8), EXPERT).reshape(experts, group)
    own_gain = jnp.sum(d_normed * scaled, axis=0)

    sent = pl.pallas_call(
        lambda *refs: dispatch_kernel(width, *refs),
        grid=(experts,),
        in_specs=[
            pl.BlockSpec((experts, group), lambda e: (0, 0)),
            pl.BlockSpec((experts, group), lambda e: (0, 0)),
            pl.BlockSpec((1, columns), lambda e: (0, 0)),
            pl.BlockSpec((experts, group), lambda e: (0, 0)),
            pl.BlockSpec((experts, group), lambda e: (0, 0)),
            pl.BlockSpec((group, columns), lambda e: (0, 0)),
            pl.BlockSpec((group, columns), lambda e: (0, 0)),
            pl.BlockSpec((group, columns), lambda e: (0, 0)),
        ],
        out_specs=pl.BlockSpec((1, capacity, columns), lambda e: (e, 0, 0)),
        out_shape=jax.ShapeDtypeStruct((experts, capacity, columns), jnp.bfloat16),
        scratch_shapes=[pltpu.VMEM((group, columns), jnp.float32)],
        compiler_params=pltpu.CompilerParams(
            dimension_semantics=("arbitrary",), vmem_limit_bytes=40 * 2**20
        ),
    )(squares, inner, norm_gain[None], slot, gate, stream_grad, attn_input, d_normed)
    arrived = lax.all_to_all(sent, EXPERT, split_axis=0, concat_axis=2, tiled=True)

    d_value = swapped(d_value, "zl").sum(axis=0)
    d_value = swapped(d_value, "zh").sum(axis=0)
    d_value = (d_value * rescale).astype(jnp.bfloat16)

    d_gain = own_gain.reshape(4, columns // 4)
    for axis in ("x", "zl", "zh"):
        d_gain = to_all(d_gain, axis).sum(axis=0)
    d_gain = d_gain.reshape(columns) * rescale
    return (d_value, d_gain, arrived)


def solution(mesh):
    split = Mesh(mesh.devices.reshape(4, 4, 4, 4, 2), ("zh", "zl", "x", "y", "core"))
    dp = ("zh", "zl", "x")
    return jax.shard_map(
        on_device,
        mesh=split,
        in_specs=(
            P(dp, EXPERT),
            P(dp + EXPERT, None),
            P(dp, EXPERT),
            P(EXPERT),
            P(dp, EXPERT),
            P(dp, None),
            P(dp, None),
        ),
        out_specs=(P(dp, EXPERT), P(EXPERT), P(EXPERT, dp, None)),
        check_vma=False,
    )
```

```python
import jax
import jax.numpy as jnp
from jax import lax
from jax.experimental import pallas as pl
from jax.experimental.pallas import tpu as pltpu
from jax.sharding import Mesh, PartitionSpec as P

epsilon = 1e-05
EXPERT = ("y", "core")


def route_kernel(routes_ref, logits_ref, slot_ref, gate_ref):
    experts, group = slot_ref.shape
    expert = lax.broadcasted_iota(jnp.int32, (experts, group), 0)
    first = routes_ref[0:1, :] == expert
    second = routes_ref[1:2, :] == expert
    named = jnp.where(first | second, 1.0, 0.0)
    earlier = lax.broadcasted_iota(jnp.int32, (group, group), 0) < lax.broadcasted_iota(
        jnp.int32, (group, group), 1
    )
    count = jnp.dot(
        named.astype(jnp.bfloat16),
        jnp.where(earlier, 1.0, 0.0).astype(jnp.bfloat16),
        preferred_element_type=jnp.float32,
    )
    slot_ref[...] = jnp.where(named > 0.0, count, -1.0).astype(jnp.int32)
    low, high = logits_ref[0:1, :], logits_ref[1:2, :]
    gate_first = 1.0 / (1.0 + jnp.exp(high - low))
    gate_second = 1.0 / (1.0 + jnp.exp(low - high))
    gate_ref[...] = jnp.where(first, gate_first, jnp.where(second, gate_second, 0.0))


def column(row):
    return jnp.transpose(jnp.broadcast_to(row, (8, row.shape[1])))[:, 0:1]


def dispatch_kernel(
    width, squares_ref, inner_ref, gain_ref, slot_ref, gate_ref, grad_ref, input_ref, normed_ref,
    out_ref, stream_ref,
):
    expert = pl.program_id(0)
    group = grad_ref.shape[0]
    capacity = out_ref.shape[1]

    @pl.when(expert == 0)
    def _():
        root_mean = jnp.sqrt(squares_ref[...] / width + epsilon)
        inner = jnp.sum(inner_ref[...], axis=0, keepdims=True) / width
        root_column, inner_column = column(root_mean), column(inner)
        scaled = input_ref[...].astype(jnp.float32) / root_column
        weighted = normed_ref[...] * gain_ref[...]
        stream_ref[...] = (
            grad_ref[...].astype(jnp.float32) + (weighted - scaled * inner_column) / root_column
        )

    slot = slot_ref[pl.ds(expert, 1), :]
    gate = column(gate_ref[pl.ds(expert, 1), :])
    rows = (gate * stream_ref[...]).astype(jnp.bfloat16)
    taken = lax.broadcasted_iota(jnp.int32, (capacity, group), 0) == slot
    picked = jnp.dot(
        jnp.where(taken, 1.0, 0.0).astype(jnp.bfloat16), rows, preferred_element_type=jnp.float32
    )
    out_ref[0] = picked.astype(jnp.bfloat16)


def to_all(part, axis):
    size = lax.axis_size(axis)
    return lax.all_to_all(
        jnp.broadcast_to(part[None], (size,) + part.shape), axis, 0, 0, tiled=True
    )


def on_device(stream_grad, value_grad, attn_input, norm_gain, value_weight, gate_logits, routes):
    group, columns = attn_input.shape
    experts = lax.axis_size(EXPERT)
    zh, zl, xs = lax.axis_size("zh"), lax.axis_size("zl"), lax.axis_size("x")
    width = columns * experts
    tokens_all = group * zh * zl * xs
    rescale = float(tokens_all) ** (-0.5)
    capacity = min(group, 5 * group // (2 * experts))
    rows = value_weight.shape[0]
    features = rows * zh * zl * xs
    vmem = pl.BlockSpec(memory_space=pltpu.VMEM)

    every_value = lax.all_gather(value_grad, EXPERT, axis=0, tiled=True)

    slot, gate = pl.pallas_call(
        route_kernel,
        in_specs=[vmem, vmem],
        out_specs=[vmem, vmem],
        out_shape=[
            jax.ShapeDtypeStruct((experts, group), jnp.int32),
            jax.ShapeDtypeStruct((experts, group), jnp.float32),
        ],
        compiler_params=pltpu.CompilerParams(vmem_limit_bytes=32 * 2**20),
    )(routes.T, gate_logits.T)

    inputs = attn_input.astype(jnp.float32)
    own_squares = jnp.sum(inputs * inputs, axis=1)
    weight = to_all(value_weight, "zh")
    weight, own_squares = lax.optimization_barrier((weight, own_squares))
    weight = to_all(weight, "zl")
    squares = lax.psum(own_squares, EXPERT)
    weight, squares = lax.optimization_barrier((weight, squares))
    weight = to_all(weight, "x")
    weight = jnp.transpose(weight, (2, 1, 0, 3, 4)).reshape(features, columns)
    root_mean = jnp.sqrt(squares / width + epsilon)[:, None]
    scaled = inputs / root_mean
    normed = (scaled * norm_gain).astype(jnp.bfloat16)

    d_value = lax.dot_general(
        every_value, normed, (((0,), (0,)), ((), ())), preferred_element_type=jnp.float32
    )
    d_value = d_value.reshape(zh, zl, xs, rows, columns).transpose(2, 1, 0, 3, 4)
    d_value = d_value.reshape(features, columns)
    for axis in ("x", "zl", "zh"):
        d_value = lax.psum_scatter(d_value, axis, scatter_dimension=0, tiled=True)
    d_value = (d_value * rescale).astype(jnp.bfloat16)

    d_normed = jnp.dot(every_value, weight, preferred_element_type=jnp.float32)
    weighted = d_normed * norm_gain
    own_inner = jnp.sum(weighted * scaled, axis=1)
    inner = to_all(own_inner.reshape(8, group // 8), EXPERT).reshape(experts, group)
    own_gain = jnp.sum(d_normed * scaled, axis=0)

    sent = pl.pallas_call(
        lambda *refs: dispatch_kernel(width, *refs),
        grid=(experts,),
        in_specs=[
            pl.BlockSpec((1, group), lambda e: (0, 0)),
            pl.BlockSpec((experts, group), lambda e: (0, 0)),
            pl.BlockSpec((1, columns), lambda e: (0, 0)),
            pl.BlockSpec((experts, group), lambda e: (0, 0)),
            pl.BlockSpec((experts, group), lambda e: (0, 0)),
            pl.BlockSpec((group, columns), lambda e: (0, 0)),
            pl.BlockSpec((group, columns), lambda e: (0, 0)),
            pl.BlockSpec((group, columns), lambda e: (0, 0)),
        ],
        out_specs=pl.BlockSpec((1, capacity, columns), lambda e: (e, 0, 0)),
        out_shape=jax.ShapeDtypeStruct((experts, capacity, columns), jnp.bfloat16),
        scratch_shapes=[pltpu.VMEM((group, columns), jnp.float32)],
        compiler_params=pltpu.CompilerParams(
            dimension_semantics=("arbitrary",), vmem_limit_bytes=40 * 2**20
        ),
    )(squares[None], inner, norm_gain[None], slot, gate, stream_grad, attn_input, d_normed)
    arrived = lax.all_to_all(sent, EXPERT, split_axis=0, concat_axis=2, tiled=True)

    d_gain = own_gain
    for axis in ("x", "zl", "zh"):
        d_gain = lax.psum(d_gain, axis)
    d_gain = d_gain * rescale
    return (d_value, d_gain, arrived)


def solution(mesh):
    split = Mesh(mesh.devices.reshape(4, 4, 4, 4, 2), ("zh", "zl", "x", "y", "core"))
    dp = ("zh", "zl", "x")
    return jax.shard_map(
        on_device,
        mesh=split,
        in_specs=(
            P(dp, EXPERT),
            P(dp + EXPERT, None),
            P(dp, EXPERT),
            P(EXPERT),
            P(dp, EXPERT),
            P(dp, None),
            P(dp, None),
        ),
        out_specs=(P(dp, EXPERT), P(EXPERT), P(EXPERT, dp, None)),
        check_vma=False,
    )
```

```python
import jax
import jax.numpy as jnp
from jax import lax
from jax.experimental import pallas as pl
from jax.experimental.pallas import tpu as pltpu
from jax.sharding import Mesh, PartitionSpec as P

epsilon = 1e-05
EXPERT = ("y", "core")
VMEM = pl.BlockSpec(memory_space=pltpu.VMEM)
SMEM = pl.BlockSpec(memory_space=pltpu.SMEM)
PAD = 16


def call(kernel, *operands, out, limit=32):
    return pl.pallas_call(
        kernel,
        in_specs=[SMEM if o.shape == (1,) else VMEM for o in operands],
        out_specs=[VMEM] * len(out),
        out_shape=[jax.ShapeDtypeStruct(shape, kind) for shape, kind in out],
        compiler_params=pltpu.CompilerParams(vmem_limit_bytes=limit * 2**20),
    )(*operands)


def column(row):
    return jnp.transpose(jnp.broadcast_to(row, (8, row.shape[1])))[:, 0:1]


def pieces(row):
    high = row.astype(jnp.bfloat16).astype(jnp.float32)
    middle = (row - high).astype(jnp.bfloat16).astype(jnp.float32)
    low = row - high - middle
    at = lax.broadcasted_iota(jnp.int32, (PAD, row.shape[1]), 0)
    rows = jnp.where(at == 0, high, jnp.where(at == 1, middle, jnp.where(at == 2, low, 0.0)))
    return rows.astype(jnp.bfloat16)


def pack_kernel(value_ref, input_ref, weight_ref, packed_ref, copies_ref):
    rows = value_ref.shape[0]
    inputs = input_ref[...].astype(jnp.float32)
    squares = jnp.sum(inputs * inputs, axis=1, keepdims=True)
    row = jnp.transpose(jnp.broadcast_to(squares, (squares.shape[0], 8)))[0:1, :]
    packed_ref[0:rows, :] = value_ref[...]
    packed_ref[rows:, :] = pieces(row)
    for peer in range(copies_ref.shape[0]):
        copies_ref[peer] = weight_ref[...]


def route_kernel(routes_ref, logits_ref, slot_ref, gate_ref):
    experts, group = slot_ref.shape
    expert = lax.broadcasted_iota(jnp.int32, (experts, group), 0)
    first = routes_ref[0:1, :] == expert
    second = routes_ref[1:2, :] == expert
    named = jnp.where(first | second, 1.0, 0.0)
    earlier = lax.broadcasted_iota(jnp.int32, (group, group), 0) < lax.broadcasted_iota(
        jnp.int32, (group, group), 1
    )
    count = jnp.dot(
        named.astype(jnp.bfloat16),
        jnp.where(earlier, 1.0, 0.0).astype(jnp.bfloat16),
        preferred_element_type=jnp.float32,
    )
    slot_ref[...] = jnp.where(named > 0.0, count, -1.0).astype(jnp.int32)
    low, high = logits_ref[0:1, :], logits_ref[1:2, :]
    gate_first = 1.0 / (1.0 + jnp.exp(high - low))
    gate_second = 1.0 / (1.0 + jnp.exp(low - high))
    gate_ref[...] = jnp.where(first, gate_first, jnp.where(second, gate_second, 0.0))


def value_kernel(width, gathered_ref, input_ref, gain_ref, d_value_ref, value_ref, inverse_ref):
    devices, packed, features = gathered_ref.shape
    rows = packed - PAD
    group = input_ref.shape[0]
    squares = jnp.zeros((1, features), jnp.float32)
    for device in range(devices):
        part = gathered_ref[device, rows:, :].astype(jnp.float32)
        squares += jnp.sum(part, axis=0, keepdims=True)
        value_ref[device * rows : (device + 1) * rows, :] = gathered_ref[device, 0:rows, :]
    inverse = 1.0 / jnp.sqrt(squares / width + epsilon)
    tile = group // 8
    for at in range(8):
        inverse_ref[at : at + 1, :] = inverse[:, at * tile : (at + 1) * tile]
    scaled = input_ref[...].astype(jnp.float32) * column(inverse)
    normed = (scaled * gain_ref[...]).astype(jnp.bfloat16)
    xs, zl, zh, own, _ = d_value_ref.shape
    block = features // zh
    for high in range(zh):
        partial = lax.dot_general(
            value_ref[:, high * block : (high + 1) * block],
            normed,
            (((0,), (0,)), ((), ())),
            preferred_element_type=jnp.float32,
        )
        for low in range(zl):
            for x in range(xs):
                start = (low * xs + x) * own
                d_value_ref[x, low, high] = partial[start : start + own, :]


def dispatch_kernel(
    width, inverse_ref, inner_ref, slot_ref, gate_ref, base_ref, input_ref, out_ref, stream_ref
):
    expert = pl.program_id(0)
    group = input_ref.shape[0]
    capacity = out_ref.shape[1]

    @pl.when(expert == 0)
    def _():
        inverse = inverse_ref[...]
        inner = jnp.sum(inner_ref[...], axis=0) / width
        factor = jnp.transpose(inner * inverse * inverse)
        tile = group // 8
        for at in range(8):
            rows = pl.ds(at * tile, tile)
            stream_ref[rows, :] = (
                base_ref[rows, :]
                - input_ref[rows, :].astype(jnp.float32) * factor[:, at : at + 1]
            )

    slot = slot_ref[pl.ds(expert, 1), :]
    gate = column(gate_ref[pl.ds(expert, 1), :])
    rows = (gate * stream_ref[...]).astype(jnp.bfloat16)
    taken = lax.broadcasted_iota(jnp.int32, (capacity, group), 0) == slot
    picked = jnp.dot(
        jnp.where(taken, 1.0, 0.0).astype(jnp.bfloat16), rows, preferred_element_type=jnp.float32
    )
    out_ref[0] = picked.astype(jnp.bfloat16)


def low_split_kernel(me_ref, d_value_ref, d_gain_ref, *outs):
    count = len(outs)
    rows = d_value_ref.shape[0] // count
    behind = pieces(d_gain_ref[...])
    for k, out in enumerate(outs):
        start = pl.multiple_of(lax.rem(me_ref[0] + k, count) * rows, rows)
        out[0:rows, :] = d_value_ref[pl.ds(start, rows), :].astype(jnp.bfloat16)
        out[rows:, :] = behind


def high_split_kernel(me_ref, a_ref, b_ref, c_ref, d_ref, sum_ref, *outs):
    count = len(outs)
    total = a_ref[...].astype(jnp.float32)
    for ref in (b_ref, c_ref, d_ref):
        total += ref[...].astype(jnp.float32)
    sum_ref[...] = total
    rows = total.shape[0] - PAD
    gain = jnp.sum(total[rows:, :], axis=0, keepdims=True)
    own = rows // count
    for k, out in enumerate(outs):
        start = pl.multiple_of(lax.rem(me_ref[0] + k, count) * own, own)
        out[0:own, :] = sum_ref[pl.ds(start, own), :]
        out[own:, :] = jnp.broadcast_to(gain, (8, gain.shape[1]))


def finish_kernel(rescale, a_ref, b_ref, c_ref, d_ref, d_value_ref, d_gain_ref):
    total = (a_ref[...] + b_ref[...]) + (c_ref[...] + d_ref[...])
    rows = d_value_ref.shape[0]
    d_value_ref[...] = (total[0:rows, :] * rescale).astype(jnp.bfloat16)
    d_gain_ref[...] = total[rows : rows + 1, :] * rescale


def to_all(part, axis):
    size = lax.axis_size(axis)
    return lax.all_to_all(
        jnp.broadcast_to(part[None], (size,) + part.shape), axis, 0, 0, tiled=True
    )


def further(part, axis, step):
    size = lax.axis_size(axis)
    return lax.ppermute(part, axis, [(i, (i + step) % size) for i in range(size)])


def on_device(stream_grad, value_grad, attn_input, norm_gain, value_weight, gate_logits, routes):
    group, columns = attn_input.shape
    experts = lax.axis_size(EXPERT)
    zh, zl, xs = lax.axis_size("zh"), lax.axis_size("zl"), lax.axis_size("x")
    width = columns * experts
    tokens_all = group * zh * zl * xs
    rescale = float(tokens_all) ** (-0.5)
    capacity = min(group, 5 * group // (2 * experts))
    rows = value_weight.shape[0]
    features = rows * zh * zl * xs
    own_rows = value_grad.shape[0]
    f32, bf16 = jnp.float32, jnp.bfloat16
    gain_row = norm_gain[None]
    me_x = lax.axis_index("x").astype(jnp.uint32)

    packed, copies = call(
        pack_kernel, value_grad, attn_input, value_weight,
        out=[((own_rows + PAD, features), bf16), ((zh, rows, columns), bf16)],
    )
    gathered = lax.all_gather(packed, EXPERT, axis=0)

    weight = to_all(lax.all_to_all(copies, "zh", 0, 0, tiled=True), "zl")
    weight = jnp.transpose(weight, (1, 0, 2, 3))
    others = [further(weight, "x", step) for step in range(1, xs)]
    gathered, others[0] = lax.optimization_barrier((gathered, others[0]))
    every_weight = jnp.zeros((zh, zl, xs, rows, columns), bf16)
    for step, part in enumerate([weight] + others):
        place = lax.rem(me_x + jnp.uint32(xs - step), jnp.uint32(xs))
        zero = jnp.uint32(0)
        every_weight = lax.dynamic_update_slice(
            every_weight, part[:, :, None], (zero, zero, place, zero, zero)
        )
    every_weight = every_weight.reshape(features, columns)

    slot, gate = call(
        route_kernel, routes.T, gate_logits.T,
        out=[((experts, group), jnp.int32), ((experts, group), f32)],
    )

    d_value, every_value, inverse = call(
        lambda *refs: value_kernel(width, *refs), gathered, attn_input, gain_row,
        out=[
            ((xs, zl, zh, rows, columns), f32),
            ((group, features), bf16),
            ((8, group // 8), f32),
        ],
        limit=40,
    )
    d_value = lax.psum_scatter(
        d_value.reshape(features, columns), "x", scatter_dimension=0, tiled=True
    )

    inverse_column = inverse.reshape(group)[:, None]
    scaled = attn_input.astype(f32) * inverse_column
    d_normed = jnp.dot(every_value, every_weight, preferred_element_type=f32)
    weighted = d_normed * norm_gain
    own_inner = jnp.sum(weighted * scaled, axis=1)
    own_gain = jnp.sum(d_normed * scaled, axis=0)
    base = stream_grad.astype(f32) + weighted * inverse_column
    inner = to_all(own_inner.reshape(8, group // 8), EXPERT)

    whole = lambda *shape: pl.BlockSpec(shape, lambda e: (0,) * len(shape))
    sent = pl.pallas_call(
        lambda *refs: dispatch_kernel(width, *refs),
        grid=(experts,),
        in_specs=[
            whole(8, group // 8),
            whole(experts, 8, group // 8),
            whole(experts, group),
            whole(experts, group),
            whole(group, columns),
            whole(group, columns),
        ],
        out_specs=pl.BlockSpec((1, capacity, columns), lambda e: (e, 0, 0)),
        out_shape=jax.ShapeDtypeStruct((experts, capacity, columns), bf16),
        scratch_shapes=[pltpu.VMEM((group, columns), f32)],
        compiler_params=pltpu.CompilerParams(
            dimension_semantics=("arbitrary",), vmem_limit_bytes=40 * 2**20
        ),
        cost_estimate=pl.CostEstimate(flops=15 * 10**9, bytes_accessed=10**7, transcendentals=0),
    )(inverse, inner, slot, gate, base, attn_input)
    sent, own_gain = lax.optimization_barrier((sent, own_gain))
    arrived = lax.all_to_all(sent, EXPERT, split_axis=0, concat_axis=2, tiled=True)

    d_gain = lax.psum(own_gain, "x")
    part = (features // xs // zl + PAD, columns)
    parts = call(
        low_split_kernel, lax.axis_index("zl").reshape(1), d_value, d_gain[None],
        out=[(part, bf16)] * zl,
    )
    parts = [parts[0]] + [further(parts[k], "zl", k) for k in range(1, zl)]
    part = (rows + 8, columns)
    _, *parts = call(
        high_split_kernel, lax.axis_index("zh").reshape(1), *parts,
        out=[(parts[0].shape, f32)] + [(part, f32)] * zh,
    )
    parts = [parts[0]] + [further(parts[k], "zh", k) for k in range(1, zh)]
    d_value, d_gain = call(
        lambda *refs: finish_kernel(rescale, *refs), *parts,
        out=[((rows, columns), bf16), ((1, columns), f32)],
    )
    return (d_value, d_gain.reshape(columns), arrived)


def solution(mesh):
    split = Mesh(mesh.devices.reshape(4, 4, 4, 4, 2), ("zh", "zl", "x", "y", "core"))
    dp = ("zh", "zl", "x")
    return jax.shard_map(
        on_device,
        mesh=split,
        in_specs=(
            P(dp, EXPERT),
            P(dp + EXPERT, None),
            P(dp, EXPERT),
            P(EXPERT),
            P(dp, EXPERT),
            P(dp, None),
            P(dp, None),
        ),
        out_specs=(P(dp, EXPERT), P(EXPERT), P(EXPERT, dp, None)),
        check_vma=False,
    )
```

```python
import jax
import jax.numpy as jnp
from jax import lax
from jax.experimental import pallas as pl
from jax.experimental.pallas import tpu as pltpu
from jax.sharding import Mesh, PartitionSpec as P

epsilon = 1e-05
EXPERT = ("y", "core")
SMEM = pl.BlockSpec(memory_space=pltpu.SMEM)
BASE_FLOPS = 4 * 10**9
SLOTS_FLOPS = 50 * 10**9
PAD = 16


def whole(shape):
    return pl.BlockSpec(shape, lambda *at: (0,) * len(shape))


def call(kernel, *operands, out, limit=60, scratch=(), grid=(1,), out_specs=None, flops=None):
    cost = {}
    if flops:
        cost["cost_estimate"] = pl.CostEstimate(
            flops=flops, bytes_accessed=10**7, transcendentals=0
        )
    return pl.pallas_call(
        kernel,
        grid=grid,
        in_specs=[SMEM if o.dtype == jnp.int32 and o.ndim == 1 else whole(o.shape) for o in operands],
        out_specs=out_specs or [whole(shape) for shape, _ in out],
        out_shape=[jax.ShapeDtypeStruct(shape, kind) for shape, kind in out],
        scratch_shapes=[pltpu.VMEM(shape, kind) for shape, kind in scratch],
        compiler_params=pltpu.CompilerParams(
            dimension_semantics=("arbitrary",) * len(grid), vmem_limit_bytes=limit * 2**20
        ),
        **cost,
    )(*operands)


def column(row):
    return jnp.transpose(jnp.broadcast_to(row, (8, row.shape[1])))[:, 0:1]


def pieces(row):
    high = row.astype(jnp.bfloat16).astype(jnp.float32)
    middle = (row - high).astype(jnp.bfloat16).astype(jnp.float32)
    low = row - high - middle
    at = lax.broadcasted_iota(jnp.int32, (PAD, row.shape[1]), 0)
    rows = jnp.where(at == 0, high, jnp.where(at == 1, middle, jnp.where(at == 2, low, 0.0)))
    return rows.astype(jnp.bfloat16)


def pack_kernel(value_ref, input_ref, weight_ref, packed_ref, copies_ref):
    rows = value_ref.shape[0]
    inputs = input_ref[...].astype(jnp.float32)
    squares = jnp.sum(inputs * inputs, axis=1, keepdims=True)
    row = jnp.transpose(jnp.broadcast_to(squares, (squares.shape[0], 8)))[0:1, :]
    packed_ref[0:rows, :] = value_ref[...]
    packed_ref[rows:, :] = pieces(row)
    for peer in range(copies_ref.shape[0]):
        copies_ref[peer] = weight_ref[...]


def route_kernel(routes_ref, logits_ref, slot_ref, gate_ref):
    experts, group = slot_ref.shape
    expert = lax.broadcasted_iota(jnp.int32, (experts, group), 0)
    first = routes_ref[0:1, :] == expert
    second = routes_ref[1:2, :] == expert
    named = jnp.where(first | second, 1.0, 0.0)
    earlier = lax.broadcasted_iota(jnp.int32, (group, group), 0) < lax.broadcasted_iota(
        jnp.int32, (group, group), 1
    )
    count = jnp.dot(
        named.astype(jnp.bfloat16),
        jnp.where(earlier, 1.0, 0.0).astype(jnp.bfloat16),
        preferred_element_type=jnp.float32,
    )
    slot_ref[...] = jnp.where(named > 0.0, count, -1.0).astype(jnp.int32)
    low, high = logits_ref[0:1, :], logits_ref[1:2, :]
    gate_first = 1.0 / (1.0 + jnp.exp(high - low))
    gate_second = 1.0 / (1.0 + jnp.exp(low - high))
    gate_ref[...] = jnp.where(first, gate_first, jnp.where(second, gate_second, 0.0))


def value_kernel(width, gathered_ref, input_ref, gain_ref, d_value_ref, inverse_ref):
    devices, packed, features = gathered_ref.shape
    rows = packed - PAD
    group = input_ref.shape[0]
    squares = jnp.zeros((1, features), jnp.float32)
    for device in range(devices):
        part = gathered_ref[device, rows:, :].astype(jnp.float32)
        squares += jnp.sum(part, axis=0, keepdims=True)
    inverse = 1.0 / jnp.sqrt(squares / width + epsilon)
    tile = group // 8
    for at in range(8):
        inverse_ref[at : at + 1, :] = inverse[:, at * tile : (at + 1) * tile]
    scaled = input_ref[...].astype(jnp.float32) * column(inverse)
    normed = (scaled * gain_ref[...]).astype(jnp.bfloat16)
    xs, zl, zh, own, _ = d_value_ref.shape
    block = features // zh
    for high in range(zh):
        partial = lax.dot_general(
            gathered_ref[:, 0:rows, high * block : (high + 1) * block].reshape(group, block),
            normed,
            (((0,), (0,)), ((), ())),
            preferred_element_type=jnp.float32,
        )
        for low in range(zl):
            for x in range(xs):
                start = (low * xs + x) * own
                d_value_ref[x, low, high] = partial[start : start + own, :]


def selected(slot_ref, rows_ref, out_ref):
    slot = slot_ref[pl.ds(pl.program_id(0), 1), :]
    taken = lax.broadcasted_iota(jnp.int32, (out_ref.shape[1], slot.shape[1]), 0) == slot
    picked = jnp.dot(
        jnp.where(taken, 1.0, 0.0).astype(jnp.bfloat16),
        rows_ref[...],
        preferred_element_type=jnp.float32,
    )
    out_ref[0] = picked.astype(jnp.bfloat16)


def base_kernel(
    me_ref, gathered_ref, input_ref, grad_ref, gain_ref, inverse_ref, slot_ref, *refs
):
    parts, (out_ref, inner_ref, d_gain_ref, weight_ref, base_ref) = refs[:-5], refs[-5:]
    devices, packed, _ = gathered_ref.shape
    rows = packed - PAD

    @pl.when(pl.program_id(0) == 0)
    def _():
        xs = len(parts)
        zl, zh, own, _ = parts[0].shape
        for x_step, part in enumerate(parts):
            x = lax.rem(me_ref[0] + (xs - x_step), xs)
            for low_step in range(zl):
                low = lax.rem(me_ref[1] + (zl - low_step), zl)
                for high in range(zh):
                    start = pl.multiple_of(((high * zl + low) * xs + x) * own, own)
                    weight_ref[pl.ds(start, own), :] = part[low_step, high]
        factor = jnp.transpose(inverse_ref[...])
        d_gain = jnp.zeros(d_gain_ref.shape, jnp.float32)
        for at in range(0, devices, 2):
            d_normed = jnp.dot(
                gathered_ref[at : at + 2, 0:rows, :].reshape(2 * rows, -1),
                weight_ref[...],
                preferred_element_type=jnp.float32,
            )
            for half in range(2):
                tokens = slice((at + half) * rows, (at + half + 1) * rows)
                normed = d_normed[half * rows : (half + 1) * rows, :]
                inverse = factor[:, at + half : at + half + 1]
                scaled = input_ref[tokens, :].astype(jnp.float32) * inverse
                weighted = normed * gain_ref[...]
                d_gain += jnp.sum(normed * scaled, axis=0, keepdims=True)
                inner = jnp.sum(weighted * scaled, axis=1, keepdims=True)
                inner = jnp.transpose(jnp.broadcast_to(inner, (rows, 8)))[0:1, :]
                inner_ref[at + half : at + half + 1, :] = inner
                base = grad_ref[tokens, :].astype(jnp.float32) + weighted * inverse
                base_ref[tokens, :] = base.astype(jnp.bfloat16)
        d_gain_ref[...] = d_gain

    selected(slot_ref, base_ref, out_ref)


def slots_kernel(width, me_ref, slot_ref, gate_ref, inverse_ref, inner_ref, gate_out, factor_out):
    capacity = gate_out.shape[0]
    tile = inverse_ref.shape[1]
    factor = inner_ref[...] / width * inverse_ref[...] * inverse_ref[...]
    slot = slot_ref[pl.ds(me_ref[0], 1), :]
    gate = gate_ref[pl.ds(me_ref[0], 1), :]
    gates = jnp.zeros((capacity, 1), jnp.float32)
    factors = jnp.zeros((capacity, 1), jnp.float32)
    for at in range(inverse_ref.shape[0]):
        tokens = slice(at * tile, (at + 1) * tile)
        taken = lax.broadcasted_iota(jnp.int32, (capacity, tile), 0) == slot[:, tokens]
        gates += jnp.sum(jnp.where(taken, gate[:, tokens], 0.0), axis=1, keepdims=True)
        factors += jnp.sum(jnp.where(taken, factor[at : at + 1, :], 0.0), axis=1, keepdims=True)
    gate_out[...] = jnp.broadcast_to(gates, gate_out.shape)
    factor_out[...] = jnp.broadcast_to(factors, factor_out.shape)


def combine_kernel(gate_ref, factor_ref, base_ref, input_ref, out_ref):
    base = base_ref[0].astype(jnp.float32)
    inputs = input_ref[0].astype(jnp.float32)
    stream = base - inputs * factor_ref[:, 0:1]
    out_ref[...] = (gate_ref[:, 0:1] * stream).astype(jnp.bfloat16)


def low_split_kernel(me_ref, d_value_ref, d_gain_ref, *outs):
    count = len(outs)
    rows = d_value_ref.shape[0] // count
    behind = pieces(d_gain_ref[...])
    for k, out in enumerate(outs):
        start = pl.multiple_of(lax.rem(me_ref[0] + k, count) * rows, rows)
        out[0:rows, :] = d_value_ref[pl.ds(start, rows), :].astype(jnp.bfloat16)
        out[rows:, :] = behind


def high_split_kernel(me_ref, a_ref, b_ref, c_ref, d_ref, sum_ref, *outs):
    count = len(outs)
    total = a_ref[...].astype(jnp.float32)
    for ref in (b_ref, c_ref, d_ref):
        total += ref[...].astype(jnp.float32)
    sum_ref[...] = total
    rows = total.shape[0] - PAD
    gain = jnp.sum(total[rows:, :], axis=0, keepdims=True)
    own = rows // count
    for k, out in enumerate(outs):
        start = pl.multiple_of(lax.rem(me_ref[0] + k, count) * own, own)
        out[0:own, :] = sum_ref[pl.ds(start, own), :]
        out[own:, :] = jnp.broadcast_to(gain, (8, gain.shape[1]))


def finish_kernel(rescale, a_ref, b_ref, c_ref, d_ref, d_value_ref, d_gain_ref):
    total = (a_ref[...] + b_ref[...]) + (c_ref[...] + d_ref[...])
    rows = d_value_ref.shape[0]
    d_value_ref[...] = (total[0:rows, :] * rescale).astype(jnp.bfloat16)
    d_gain_ref[...] = total[rows : rows + 1, :] * rescale


def further(part, axis, step):
    size = lax.axis_size(axis)
    return lax.ppermute(part, axis, [(i, (i + step) % size) for i in range(size)])


def on_device(stream_grad, value_grad, attn_input, norm_gain, value_weight, gate_logits, routes):
    group, columns = attn_input.shape
    experts = lax.axis_size(EXPERT)
    zh, zl, xs = lax.axis_size("zh"), lax.axis_size("zl"), lax.axis_size("x")
    width = columns * experts
    tokens_all = group * zh * zl * xs
    rescale = float(tokens_all) ** (-0.5)
    capacity = min(group, 5 * group // (2 * experts))
    rows = value_weight.shape[0]
    features = rows * zh * zl * xs
    own_rows = value_grad.shape[0]
    f32, bf16 = jnp.float32, jnp.bfloat16
    gain_row = norm_gain[None]

    packed, copies = call(
        pack_kernel, value_grad, attn_input, value_weight,
        out=[((own_rows + PAD, features), bf16), ((zh, rows, columns), bf16)],
    )
    gathered = lax.all_gather(packed, EXPERT, axis=0)
    slot, gate = call(
        route_kernel, routes.T, gate_logits.T,
        out=[((experts, group), jnp.int32), ((experts, group), f32)],
    )
    by_slot = ((experts, capacity, columns), bf16)
    one_slot_block = pl.BlockSpec((1, capacity, columns), lambda e: (e, 0, 0))
    (input_rows,) = call(
        selected, slot, attn_input, out=[by_slot], out_specs=[one_slot_block], grid=(experts,)
    )

    weight = lax.all_to_all(copies, "zh", 0, 0, tiled=True)
    weight, input_rows = lax.optimization_barrier((weight, input_rows))
    input_rows = lax.all_to_all(input_rows, EXPERT, 0, 0, tiled=True)
    weight = jnp.stack([weight] + [further(weight, "zl", step) for step in range(1, zl)])
    weights = [weight] + [further(weight, "x", step) for step in range(1, xs)]
    gathered, weights[1] = lax.optimization_barrier((gathered, weights[1]))

    d_value, inverse = call(
        lambda *refs: value_kernel(width, *refs), gathered, attn_input, gain_row,
        out=[((xs, zl, zh, rows, columns), f32), ((8, group // 8), f32)],
    )
    d_value = lax.psum_scatter(
        d_value.reshape(features, columns), "x", scatter_dimension=0, tiled=True
    )

    sent, inner, own_gain = call(
        base_kernel, jnp.stack([lax.axis_index("x"), lax.axis_index("zl")]),
        gathered, attn_input, stream_grad, gain_row, inverse, slot, *weights,
        out=[by_slot, ((8, group // 8), f32), ((1, columns), f32)],
        out_specs=[one_slot_block, whole((8, group // 8)), whole((1, columns))],
        scratch=[((features, columns), bf16), ((group, columns), bf16)],
        grid=(experts,),
        flops=BASE_FLOPS,
    )
    sent, inner, own_gain = lax.optimization_barrier((sent, inner, own_gain))
    arrived = lax.all_to_all(sent, EXPERT, 0, 0, tiled=True)

    d_gain = lax.psum(own_gain, "x")
    inner = lax.psum(inner, EXPERT)
    lanes = ((capacity, 128), f32)
    slot_gate, slot_factor = call(
        lambda *refs: slots_kernel(width, *refs), lax.axis_index(EXPERT).reshape(1),
        slot, gate, inverse, inner, out=[lanes, lanes], flops=SLOTS_FLOPS,
    )
    block = pl.BlockSpec((1, capacity, columns), lambda d: (d, 0, 0))
    dispatched = pl.pallas_call(
        combine_kernel,
        grid=(experts,),
        in_specs=[whole(lanes[0]), whole(lanes[0]), block, block],
        out_specs=pl.BlockSpec((capacity, columns), lambda d: (0, d)),
        out_shape=jax.ShapeDtypeStruct((capacity, width), bf16),
        compiler_params=pltpu.CompilerParams(
            dimension_semantics=("arbitrary",), vmem_limit_bytes=40 * 2**20
        ),
    )(slot_gate, slot_factor, arrived, input_rows)

    d_gain, _ = lax.optimization_barrier((d_gain, slot_gate))
    part = (features // xs // zl + PAD, columns)
    parts = call(
        low_split_kernel, lax.axis_index("zl").reshape(1), d_value, d_gain,
        out=[(part, bf16)] * zl,
    )
    parts = [parts[0]] + [further(parts[k], "zl", k) for k in range(1, zl)]
    part = (rows + 8, columns)
    _, *parts = call(
        high_split_kernel, lax.axis_index("zh").reshape(1), *parts,
        out=[(parts[0].shape, f32)] + [(part, f32)] * zh,
    )
    parts = [parts[0]] + [further(parts[k], "zh", k) for k in range(1, zh)]
    d_value, d_gain = call(
        lambda *refs: finish_kernel(rescale, *refs), *parts,
        out=[((rows, columns), bf16), ((1, columns), f32)],
    )
    return (d_value, d_gain.reshape(columns), dispatched[None])


def solution(mesh):
    split = Mesh(mesh.devices.reshape(4, 4, 4, 4, 2), ("zh", "zl", "x", "y", "core"))
    dp = ("zh", "zl", "x")
    return jax.shard_map(
        on_device,
        mesh=split,
        in_specs=(
            P(dp, EXPERT),
            P(dp + EXPERT, None),
            P(dp, EXPERT),
            P(EXPERT),
            P(dp, EXPERT),
            P(dp, None),
            P(dp, None),
        ),
        out_specs=(P(dp, EXPERT), P(EXPERT), P(EXPERT, dp, None)),
        check_vma=False,
    )
```

```python
import jax
import jax.numpy as jnp
from jax import lax
from jax.experimental import pallas as pl
from jax.experimental.pallas import tpu as pltpu
from jax.sharding import Mesh, PartitionSpec as P

epsilon = 1e-05
EXPERT = ("y", "core")
SMEM = pl.BlockSpec(memory_space=pltpu.SMEM)
PAD = 16
NORMED_FLOPS = 4 * 10**9
DISPATCH_FLOPS = 20 * 10**9


def whole(shape):
    return pl.BlockSpec(shape, lambda *at: (0,) * len(shape))


def call(
    kernel, *operands, out, limit=60, grid=1, scratch=(), in_specs=None, out_specs=None, flops=None
):
    cost = {}
    if flops:
        cost["cost_estimate"] = pl.CostEstimate(
            flops=flops, bytes_accessed=10**7, transcendentals=0
        )
    return pl.pallas_call(
        kernel,
        grid=(grid,),
        in_specs=in_specs or [SMEM if o.shape == (1,) else whole(o.shape) for o in operands],
        out_specs=out_specs or [whole(shape) for shape, _ in out],
        out_shape=[jax.ShapeDtypeStruct(shape, kind) for shape, kind in out],
        scratch_shapes=[pltpu.VMEM(shape, kind) for shape, kind in scratch],
        compiler_params=pltpu.CompilerParams(
            dimension_semantics=("arbitrary",), vmem_limit_bytes=limit * 2**20
        ),
        **cost,
    )(*operands)


def column(row):
    return jnp.transpose(jnp.broadcast_to(row, (8, row.shape[1])))[:, 0:1]


def pieces(row):
    high = row.astype(jnp.bfloat16).astype(jnp.float32)
    middle = (row - high).astype(jnp.bfloat16).astype(jnp.float32)
    low = row - high - middle
    at = lax.broadcasted_iota(jnp.int32, (PAD, row.shape[1]), 0)
    rows = jnp.where(at == 0, high, jnp.where(at == 1, middle, jnp.where(at == 2, low, 0.0)))
    return rows.astype(jnp.bfloat16)


def pack_kernel(value_ref, input_ref, weight_ref, packed_ref, copies_ref):
    rows = value_ref.shape[0]
    inputs = input_ref[...].astype(jnp.float32)
    squares = jnp.sum(inputs * inputs, axis=1, keepdims=True)
    row = jnp.transpose(jnp.broadcast_to(squares, (squares.shape[0], 8)))[0:1, :]
    packed_ref[0:rows, :] = value_ref[...]
    packed_ref[rows:, :] = pieces(row)
    for peer in range(copies_ref.shape[0]):
        copies_ref[peer] = weight_ref[...]


def route_kernel(routes_ref, logits_ref, slot_ref, gate_ref):
    experts, group = slot_ref.shape
    expert = lax.broadcasted_iota(jnp.int32, (experts, group), 0)
    first = routes_ref[0:1, :] == expert
    second = routes_ref[1:2, :] == expert
    named = jnp.where(first | second, 1.0, 0.0)
    earlier = lax.broadcasted_iota(jnp.int32, (group, group), 0) < lax.broadcasted_iota(
        jnp.int32, (group, group), 1
    )
    count = jnp.dot(
        named.astype(jnp.bfloat16),
        jnp.where(earlier, 1.0, 0.0).astype(jnp.bfloat16),
        preferred_element_type=jnp.float32,
    )
    slot_ref[...] = jnp.where(named > 0.0, count, -1.0).astype(jnp.int32)
    low, high = logits_ref[0:1, :], logits_ref[1:2, :]
    gate_first = 1.0 / (1.0 + jnp.exp(high - low))
    gate_second = 1.0 / (1.0 + jnp.exp(low - high))
    gate_ref[...] = jnp.where(first, gate_first, jnp.where(second, gate_second, 0.0))


def value_kernel(
    width, squares_ref, value_ref, input_ref, gain_ref, d_value_ref, inverse_ref, normed_ref
):
    group = input_ref.shape[0]

    @pl.when(pl.program_id(0) == 0)
    def _():
        squares = jnp.zeros((1, group), jnp.float32)
        for device in range(squares_ref.shape[0]):
            part = squares_ref[device].astype(jnp.float32)
            squares += jnp.sum(part, axis=0, keepdims=True)
        inverse = 1.0 / jnp.sqrt(squares / width + epsilon)
        tile = group // 8
        for at in range(8):
            inverse_ref[at : at + 1, :] = inverse[:, at * tile : (at + 1) * tile]
        scaled = input_ref[...].astype(jnp.float32) * column(inverse)
        normed_ref[...] = (scaled * gain_ref[...]).astype(jnp.bfloat16)

    xs, zl, _, own, _ = d_value_ref.shape
    partial = lax.dot_general(
        value_ref[...].reshape(group, -1),
        normed_ref[...],
        (((0,), (0,)), ((), ())),
        preferred_element_type=jnp.float32,
    )
    for low in range(zl):
        for x in range(xs):
            start = (low * xs + x) * own
            d_value_ref[x, low, 0] = partial[start : start + own, :]


def normed_kernel(
    me_ref, value_ref, input_ref, grad_ref, gain_ref, inverse_ref, *refs
):
    parts, (base_ref, inner_ref, d_gain_ref, weight_ref) = refs[:-4], refs[-4:]
    step = pl.program_id(0)

    @pl.when(step == 0)
    def _():
        xs = len(parts)
        zl, zh, own, _ = parts[0].shape
        for x_step, part in enumerate(parts):
            x = lax.rem(me_ref[0] + (xs - x_step), xs)
            for low in range(zl):
                for high in range(zh):
                    start = pl.multiple_of(((high * zl + low) * xs + x) * own, own)
                    weight_ref[pl.ds(start, own), :] = part[low, high]
        d_gain_ref[...] = jnp.zeros(d_gain_ref.shape, jnp.float32)

    devices, rows, features = value_ref.shape
    d_normed = jnp.dot(
        value_ref[...].reshape(devices * rows, features),
        weight_ref[...],
        preferred_element_type=jnp.float32,
    )
    d_gain = d_gain_ref[...]
    for at in range(devices):
        tokens = slice(at * rows, (at + 1) * rows)
        inverse = column(inverse_ref[pl.ds(step * devices + at, 1), :])
        normed = d_normed[tokens, :]
        scaled = input_ref[tokens, :].astype(jnp.float32) * inverse
        weighted = normed * gain_ref[...]
        d_gain += jnp.sum(normed * scaled, axis=0, keepdims=True)
        inner = jnp.sum(weighted * scaled, axis=1, keepdims=True)
        inner = jnp.transpose(jnp.broadcast_to(inner, (rows, 8)))[0:1, :]
        for peer in range(inner_ref.shape[0]):
            inner_ref[peer, pl.ds(step * devices + at, 1), :] = inner
        base_ref[tokens, :] = grad_ref[tokens, :].astype(jnp.float32) + weighted * inverse
    d_gain_ref[...] = d_gain


def dispatch_kernel(
    width, inverse_ref, inner_ref, slot_ref, gate_ref, base_ref, input_ref, out_ref, stream_ref
):
    step = pl.program_id(0)
    group = input_ref.shape[0]
    experts, capacity, _ = out_ref.shape

    @pl.when(step == 0)
    def _():
        inverse = inverse_ref[...]
        inner = jnp.sum(inner_ref[...], axis=0) / width
        factor = jnp.transpose(inner * inverse * inverse)
        tile = group // 8
        for at in range(8):
            rows = pl.ds(at * tile, tile)
            stream = (
                base_ref[rows, :]
                - input_ref[rows, :].astype(jnp.float32) * factor[:, at : at + 1]
            )
            stream_ref[rows, :] = stream.astype(jnp.bfloat16)

    for at in range(experts):
        slot = slot_ref[pl.ds(step * experts + at, 1), :]
        gate = gate_ref[pl.ds(step * experts + at, 1), :]
        taken = lax.broadcasted_iota(jnp.int32, (capacity, group), 0) == slot
        gates = jnp.sum(jnp.where(taken, gate, 0.0), axis=1, keepdims=True)
        picked = jnp.dot(
            jnp.where(taken, 1.0, 0.0).astype(jnp.bfloat16),
            stream_ref[...],
            preferred_element_type=jnp.float32,
        )
        out_ref[at] = (gates * picked).astype(jnp.bfloat16)


def low_split_kernel(me_ref, d_value_ref, d_gain_ref, *outs):
    count = len(outs)
    rows = d_value_ref.shape[0] // count
    behind = pieces(d_gain_ref[...])
    for k, out in enumerate(outs):
        start = pl.multiple_of(lax.rem(me_ref[0] + k, count) * rows, rows)
        out[0:rows, :] = d_value_ref[pl.ds(start, rows), :].astype(jnp.bfloat16)
        out[rows:, :] = behind


def high_split_kernel(me_ref, a_ref, b_ref, c_ref, d_ref, sum_ref, *outs):
    count = len(outs)
    total = a_ref[...].astype(jnp.float32)
    for ref in (b_ref, c_ref, d_ref):
        total += ref[...].astype(jnp.float32)
    sum_ref[...] = total
    rows = total.shape[0] - PAD
    gain = jnp.sum(total[rows:, :], axis=0, keepdims=True)
    own = rows // count
    for k, out in enumerate(outs):
        start = pl.multiple_of(lax.rem(me_ref[0] + k, count) * own, own)
        out[0:own, :] = sum_ref[pl.ds(start, own), :]
        out[own:, :] = jnp.broadcast_to(gain, (8, gain.shape[1]))


def finish_kernel(rescale, a_ref, b_ref, c_ref, d_ref, d_value_ref, d_gain_ref):
    total = (a_ref[...] + b_ref[...]) + (c_ref[...] + d_ref[...])
    rows = d_value_ref.shape[0]
    d_value_ref[...] = (total[0:rows, :] * rescale).astype(jnp.bfloat16)
    d_gain_ref[...] = total[rows : rows + 1, :] * rescale


def to_all(part, axis):
    size = lax.axis_size(axis)
    return lax.all_to_all(
        jnp.broadcast_to(part[None], (size,) + part.shape), axis, 0, 0, tiled=True
    )


def further(part, axis, step):
    size = lax.axis_size(axis)
    return lax.ppermute(part, axis, [(i, (i + step) % size) for i in range(size)])


def on_device(stream_grad, value_grad, attn_input, norm_gain, value_weight, gate_logits, routes):
    group, columns = attn_input.shape
    experts = lax.axis_size(EXPERT)
    zh, zl, xs = lax.axis_size("zh"), lax.axis_size("zl"), lax.axis_size("x")
    width = columns * experts
    tokens_all = group * zh * zl * xs
    rescale = float(tokens_all) ** (-0.5)
    capacity = min(group, 5 * group // (2 * experts))
    rows = value_weight.shape[0]
    features = rows * zh * zl * xs
    own_rows = value_grad.shape[0]
    f32, bf16 = jnp.float32, jnp.bfloat16
    gain_row = norm_gain[None]

    packed, copies = call(
        pack_kernel, value_grad, attn_input, value_weight,
        out=[((own_rows + PAD, features), bf16), ((zh, rows, columns), bf16)],
    )
    gathered = lax.all_gather(packed, EXPERT, axis=0)

    weight = to_all(lax.all_to_all(copies, "zh", 0, 0, tiled=True), "zl")
    weights = [weight] + [further(weight, "x", step) for step in range(1, xs)]
    gathered, weights[1] = lax.optimization_barrier((gathered, weights[1]))

    slot, gate = call(
        route_kernel, routes.T, gate_logits.T,
        out=[((experts, group), jnp.int32), ((experts, group), f32)],
    )

    block = features // zh
    d_value, inverse = call(
        lambda *refs: value_kernel(width, *refs), gathered, gathered, attn_input, gain_row,
        out=[((xs, zl, zh, rows, columns), f32), ((8, group // 8), f32)],
        in_specs=[
            pl.BlockSpec((experts, PAD, features), lambda i: (0, own_rows // PAD, 0)),
            pl.BlockSpec((experts, own_rows, block), lambda i: (0, 0, i)),
            whole((group, columns)),
            whole((1, columns)),
        ],
        out_specs=[
            pl.BlockSpec((xs, zl, 1, rows, columns), lambda i: (0, 0, i, 0, 0)),
            whole((8, group // 8)),
        ],
        scratch=[((group, columns), bf16)],
        grid=zh,
    )
    d_value = lax.psum_scatter(
        d_value.reshape(features, columns), "x", scatter_dimension=0, tiled=True
    )

    two = pl.BlockSpec((2 * own_rows, columns), lambda i: (i, 0))
    base, inner, own_gain = call(
        normed_kernel, lax.axis_index("x").reshape(1), gathered, attn_input, stream_grad,
        gain_row, inverse, *weights,
        out=[((group, columns), f32), ((experts, 8, group // 8), f32), ((1, columns), f32)],
        in_specs=[
            SMEM,
            pl.BlockSpec((2, own_rows, features), lambda i: (i, 0, 0)),
            two,
            two,
            whole((1, columns)),
            whole((8, group // 8)),
        ]
        + [whole(part.shape) for part in weights],
        out_specs=[two, whole((experts, 8, group // 8)), whole((1, columns))],
        scratch=[((features, columns), bf16)],
        grid=experts // 2,
        limit=40,
        flops=NORMED_FLOPS,
    )
    inner = lax.all_to_all(inner, EXPERT, 0, 0, tiled=True)

    (sent,) = call(
        lambda *refs: dispatch_kernel(width, *refs),
        inverse, inner, slot, gate, base, attn_input,
        out=[((experts, capacity, columns), bf16)],
        out_specs=[pl.BlockSpec((experts // 4, capacity, columns), lambda e: (e, 0, 0))],
        scratch=[((group, columns), bf16)],
        grid=4,
        flops=DISPATCH_FLOPS,
    )
    sent, own_gain = lax.optimization_barrier((sent, own_gain))
    arrived = lax.all_to_all(sent, EXPERT, split_axis=0, concat_axis=2, tiled=True)

    d_gain = lax.psum(own_gain, "x")
    part = (features // xs // zl + PAD, columns)
    parts = call(
        low_split_kernel, lax.axis_index("zl").reshape(1), d_value, d_gain,
        out=[(part, bf16)] * zl, limit=8,
    )
    parts = [parts[0]] + [further(parts[k], "zl", k) for k in range(1, zl)]
    part = (rows + 8, columns)
    _, *parts = call(
        high_split_kernel, lax.axis_index("zh").reshape(1), *parts,
        out=[(parts[0].shape, f32)] + [(part, f32)] * zh, limit=8,
    )
    parts = [parts[0]] + [further(parts[k], "zh", k) for k in range(1, zh)]
    d_value, d_gain = call(
        lambda *refs: finish_kernel(rescale, *refs), *parts,
        out=[((rows, columns), bf16), ((1, columns), f32)], limit=8,
    )
    return (d_value, d_gain.reshape(columns), arrived)


def solution(mesh):
    split = Mesh(mesh.devices.reshape(4, 4, 4, 4, 2), ("zh", "zl", "x", "y", "core"))
    dp = ("zh", "zl", "x")
    return jax.shard_map(
        on_device,
        mesh=split,
        in_specs=(
            P(dp, EXPERT),
            P(dp + EXPERT, None),
            P(dp, EXPERT),
            P(EXPERT),
            P(dp, EXPERT),
            P(dp, None),
            P(dp, None),
        ),
        out_specs=(P(dp, EXPERT), P(EXPERT), P(EXPERT, dp, None)),
        check_vma=False,
    )
```

```python
import jax
import jax.numpy as jnp
from jax import lax
from jax.experimental import pallas as pl
from jax.experimental.pallas import tpu as pltpu
from jax.sharding import Mesh, PartitionSpec as P

epsilon = 1e-05
EXPERT = ("y", "core")
ANY = pl.BlockSpec(memory_space=pl.ANY)
SMEM = pl.BlockSpec(memory_space=pltpu.SMEM)
PAD = 16
VALUE_LIMIT = 62
NORMED_LIMIT = 52
NORMED_FLOPS = 4 * 10**9
DISPATCH_FLOPS = 20 * 10**9


def whole(shape):
    return pl.BlockSpec(shape, lambda *at: (0,) * len(shape))


def call(
    kernel, *operands, out, limit=60, grid=1, scratch=(), in_specs=None, out_specs=None, flops=None
):
    cost = {}
    if flops:
        cost["cost_estimate"] = pl.CostEstimate(
            flops=flops, bytes_accessed=10**7, transcendentals=0
        )
    return pl.pallas_call(
        kernel,
        grid=(grid,),
        in_specs=in_specs or [SMEM if o.shape == (1,) else whole(o.shape) for o in operands],
        out_specs=out_specs or [whole(shape) for shape, _ in out],
        out_shape=[jax.ShapeDtypeStruct(shape, kind) for shape, kind in out],
        scratch_shapes=scratch,
        compiler_params=pltpu.CompilerParams(
            dimension_semantics=("arbitrary",), vmem_limit_bytes=limit * 2**20
        ),
        **cost,
    )(*operands)


def column(row):
    return jnp.transpose(jnp.broadcast_to(row, (8, row.shape[1])))[:, 0:1]


def pieces(row):
    high = row.astype(jnp.bfloat16).astype(jnp.float32)
    middle = (row - high).astype(jnp.bfloat16).astype(jnp.float32)
    low = row - high - middle
    at = lax.broadcasted_iota(jnp.int32, (PAD, row.shape[1]), 0)
    rows = jnp.where(at == 0, high, jnp.where(at == 1, middle, jnp.where(at == 2, low, 0.0)))
    return rows.astype(jnp.bfloat16)


def pack_kernel(value_ref, input_ref, weight_ref, packed_ref, copies_ref):
    rows = value_ref.shape[0]
    inputs = input_ref[...].astype(jnp.float32)
    squares = jnp.sum(inputs * inputs, axis=1, keepdims=True)
    row = jnp.transpose(jnp.broadcast_to(squares, (squares.shape[0], 8)))[0:1, :]
    packed_ref[0:rows, :] = value_ref[...]
    packed_ref[rows:, :] = pieces(row)
    for peer in range(copies_ref.shape[0]):
        copies_ref[peer] = weight_ref[...]


def route_kernel(routes_ref, logits_ref, slot_ref, gate_ref):
    experts, group = slot_ref.shape
    expert = lax.broadcasted_iota(jnp.int32, (experts, group), 0)
    first = routes_ref[0:1, :] == expert
    second = routes_ref[1:2, :] == expert
    named = jnp.where(first | second, 1.0, 0.0)
    earlier = lax.broadcasted_iota(jnp.int32, (group, group), 0) < lax.broadcasted_iota(
        jnp.int32, (group, group), 1
    )
    count = jnp.dot(
        named.astype(jnp.bfloat16),
        jnp.where(earlier, 1.0, 0.0).astype(jnp.bfloat16),
        preferred_element_type=jnp.float32,
    )
    slot_ref[...] = jnp.where(named > 0.0, count, -1.0).astype(jnp.int32)
    low, high = logits_ref[0:1, :], logits_ref[1:2, :]
    gate_first = 1.0 / (1.0 + jnp.exp(high - low))
    gate_second = 1.0 / (1.0 + jnp.exp(low - high))
    gate_ref[...] = jnp.where(first, gate_first, jnp.where(second, gate_second, 0.0))


def value_kernel(
    width, gathered_ref, whole_input_ref, gain_ref, d_value_ref, inverse_ref,
    squares_ref, input_ref, value_ref, normed_ref, partial_ref, sems,
):
    devices, rows, features = value_ref.shape
    group = input_ref.shape[0]
    get_squares = pltpu.make_async_copy(
        gathered_ref.at[:, pl.ds(rows, PAD), :], squares_ref, sems.at[0]
    )
    get_value = pltpu.make_async_copy(
        gathered_ref.at[:, pl.ds(0, rows), :], value_ref, sems.at[1]
    )
    get_input = pltpu.make_async_copy(whole_input_ref, input_ref, sems.at[2])
    get_squares.start()
    get_input.start()
    get_value.start()
    get_squares.wait()
    squares = jnp.zeros((1, group), jnp.float32)
    for device in range(devices):
        part = squares_ref[device].astype(jnp.float32)
        squares += jnp.sum(part, axis=0, keepdims=True)
    inverse = 1.0 / jnp.sqrt(squares / width + epsilon)
    tile = group // 8
    for at in range(8):
        inverse_ref[at : at + 1, :] = inverse[:, at * tile : (at + 1) * tile]
    get_input.wait()
    scaled = input_ref[...].astype(jnp.float32) * column(inverse)
    normed_ref[...] = (scaled * gain_ref[...]).astype(jnp.bfloat16)

    zh, xs, zl, own, _ = partial_ref.shape
    block = features // zh
    get_value.wait()
    puts = []
    for high in range(zh):
        partial = lax.dot_general(
            value_ref[:, :, high * block : (high + 1) * block].reshape(group, block),
            normed_ref[...],
            (((0,), (0,)), ((), ())),
            preferred_element_type=jnp.float32,
        )
        for low in range(zl):
            for x in range(xs):
                start = (low * xs + x) * own
                partial_ref[high, x, low] = partial[start : start + own, :]
        put = pltpu.make_async_copy(
            partial_ref.at[high], d_value_ref.at[:, :, high], sems.at[3 + high]
        )
        put.start()
        puts.append(put)
    for put in puts:
        put.wait()


def normed_kernel(
    me_ref, value_ref, input_ref, grad_ref, gain_ref, inverse_ref, *refs
):
    parts, (base_ref, inner_ref, d_gain_ref, weight_ref, sems) = refs[:-5], refs[-5:]
    step = pl.program_id(0)

    @pl.when(step == 0)
    def _():
        xs, zl = len(parts), parts[0].shape[0]
        gets = []
        for x_step, part in enumerate(parts):
            x = lax.rem(me_ref[0] + (xs - x_step), xs)
            for low in range(zl):
                get = pltpu.make_async_copy(
                    part.at[low], weight_ref.at[:, low, x], sems.at[x_step, low]
                )
                get.start()
                gets.append(get)
        d_gain_ref[...] = jnp.zeros(d_gain_ref.shape, jnp.float32)
        for get in gets:
            get.wait()

    devices, rows, features = value_ref.shape
    d_normed = jnp.dot(
        value_ref[...].reshape(devices * rows, features),
        weight_ref[...].reshape(features, -1),
        preferred_element_type=jnp.float32,
    )
    d_gain = d_gain_ref[...]
    for at in range(devices):
        tokens = slice(at * rows, (at + 1) * rows)
        inverse = column(inverse_ref[pl.ds(step * devices + at, 1), :])
        normed = d_normed[tokens, :]
        scaled = input_ref[tokens, :].astype(jnp.float32) * inverse
        weighted = normed * gain_ref[...]
        d_gain += jnp.sum(normed * scaled, axis=0, keepdims=True)
        inner = jnp.sum(weighted * scaled, axis=1, keepdims=True)
        inner = jnp.transpose(jnp.broadcast_to(inner, (rows, 8)))[0:1, :]
        for peer in range(inner_ref.shape[0]):
            inner_ref[peer, pl.ds(step * devices + at, 1), :] = inner
        base_ref[tokens, :] = grad_ref[tokens, :].astype(jnp.float32) + weighted * inverse
    d_gain_ref[...] = d_gain


def dispatch_kernel(
    width, inverse_ref, inner_ref, slot_ref, gate_ref, base_ref, input_ref, out_ref, stream_ref
):
    step = pl.program_id(0)
    group = input_ref.shape[0]
    experts, capacity, _ = out_ref.shape

    @pl.when(step == 0)
    def _():
        inverse = inverse_ref[...]
        inner = jnp.sum(inner_ref[...], axis=0) / width
        factor = jnp.transpose(inner * inverse * inverse)
        tile = group // 8
        for at in range(8):
            rows = pl.ds(at * tile, tile)
            stream = (
                base_ref[rows, :]
                - input_ref[rows, :].astype(jnp.float32) * factor[:, at : at + 1]
            )
            stream_ref[rows, :] = stream.astype(jnp.bfloat16)

    for at in range(experts):
        slot = slot_ref[pl.ds(step * experts + at, 1), :]
        gate = gate_ref[pl.ds(step * experts + at, 1), :]
        taken = lax.broadcasted_iota(jnp.int32, (capacity, group), 0) == slot
        gates = jnp.sum(jnp.where(taken, gate, 0.0), axis=1, keepdims=True)
        picked = jnp.dot(
            jnp.where(taken, 1.0, 0.0).astype(jnp.bfloat16),
            stream_ref[...],
            preferred_element_type=jnp.float32,
        )
        out_ref[at] = (gates * picked).astype(jnp.bfloat16)


def low_split_kernel(me_ref, d_value_ref, d_gain_ref, *outs):
    count = len(outs)
    rows = d_value_ref.shape[0] // count
    behind = pieces(d_gain_ref[...])
    for k, out in enumerate(outs):
        start = pl.multiple_of(lax.rem(me_ref[0] + k, count) * rows, rows)
        out[0:rows, :] = d_value_ref[pl.ds(start, rows), :].astype(jnp.bfloat16)
        out[rows:, :] = behind


def high_split_kernel(a_ref, b_ref, c_ref, d_ref, out_ref):
    total = a_ref[...].astype(jnp.float32)
    for ref in (b_ref, c_ref, d_ref):
        total += ref[...].astype(jnp.float32)
    rows = total.shape[0] - PAD
    gain = jnp.sum(total[rows:, :], axis=0, keepdims=True)
    own = rows // out_ref.shape[0]
    for at in range(out_ref.shape[0]):
        out_ref[at, 0:own, :] = total[at * own : (at + 1) * own, :]
        out_ref[at, own:, :] = jnp.broadcast_to(gain, (8, gain.shape[1]))


def finish_kernel(rescale, parts_ref, d_value_ref, d_gain_ref):
    total = jnp.sum(parts_ref[...], axis=0)
    rows = d_value_ref.shape[0]
    d_value_ref[...] = (total[0:rows, :] * rescale).astype(jnp.bfloat16)
    d_gain_ref[...] = total[rows : rows + 1, :] * rescale


def to_all(part, axis):
    size = lax.axis_size(axis)
    return lax.all_to_all(
        jnp.broadcast_to(part[None], (size,) + part.shape), axis, 0, 0, tiled=True
    )


def further(part, axis, step):
    size = lax.axis_size(axis)
    return lax.ppermute(part, axis, [(i, (i + step) % size) for i in range(size)])


def on_device(stream_grad, value_grad, attn_input, norm_gain, value_weight, gate_logits, routes):
    group, columns = attn_input.shape
    experts = lax.axis_size(EXPERT)
    zh, zl, xs = lax.axis_size("zh"), lax.axis_size("zl"), lax.axis_size("x")
    width = columns * experts
    tokens_all = group * zh * zl * xs
    rescale = float(tokens_all) ** (-0.5)
    capacity = min(group, 5 * group // (2 * experts))
    rows = value_weight.shape[0]
    features = rows * zh * zl * xs
    own_rows = value_grad.shape[0]
    f32, bf16 = jnp.float32, jnp.bfloat16
    gain_row = norm_gain[None]

    packed, copies = call(
        pack_kernel, value_grad, attn_input, value_weight,
        out=[((own_rows + PAD, features), bf16), ((zh, rows, columns), bf16)],
    )
    gathered = lax.all_gather(packed, EXPERT, axis=0)

    weight = to_all(lax.all_to_all(copies, "zh", 0, 0, tiled=True), "zl")
    weights = [weight] + [further(weight, "x", step) for step in range(1, xs)]
    gathered, weights[1] = lax.optimization_barrier((gathered, weights[1]))

    slot, gate = call(
        route_kernel, routes.T, gate_logits.T,
        out=[((experts, group), jnp.int32), ((experts, group), f32)],
    )

    d_value, inverse = call(
        lambda *refs: value_kernel(width, *refs), gathered, attn_input, gain_row,
        out=[((xs, zl, zh, rows, columns), f32), ((8, group // 8), f32)],
        in_specs=[ANY, ANY, whole((1, columns))],
        out_specs=[ANY, whole((8, group // 8))],
        scratch=[
            pltpu.VMEM((experts, PAD, features), bf16),
            pltpu.VMEM((group, columns), bf16),
            pltpu.VMEM((experts, own_rows, features), bf16),
            pltpu.VMEM((group, columns), bf16),
            pltpu.VMEM((zh, xs, zl, rows, columns), f32),
            pltpu.SemaphoreType.DMA((3 + zh,)),
        ],
        limit=VALUE_LIMIT,
    )
    d_value = lax.psum_scatter(
        d_value.reshape(features, columns), "x", scatter_dimension=0, tiled=True
    )

    two = pl.BlockSpec((2 * own_rows, columns), lambda i: (i, 0))
    base, inner, own_gain = call(
        normed_kernel, lax.axis_index("x").reshape(1), gathered, attn_input, stream_grad,
        gain_row, inverse, *weights,
        out=[((group, columns), f32), ((experts, 8, group // 8), f32), ((1, columns), f32)],
        in_specs=[
            SMEM,
            pl.BlockSpec((2, own_rows, features), lambda i: (i, 0, 0)),
            two,
            two,
            whole((1, columns)),
            whole((8, group // 8)),
        ]
        + [ANY] * xs,
        out_specs=[two, whole((experts, 8, group // 8)), whole((1, columns))],
        scratch=[
            pltpu.VMEM((zh, zl, xs, rows, columns), bf16),
            pltpu.SemaphoreType.DMA((xs, zl)),
        ],
        grid=experts // 2,
        limit=NORMED_LIMIT,
        flops=NORMED_FLOPS,
    )
    inner = lax.all_to_all(inner, EXPERT, 0, 0, tiled=True)

    (sent,) = call(
        lambda *refs: dispatch_kernel(width, *refs),
        inverse, inner, slot, gate, base, attn_input,
        out=[((experts, capacity, columns), bf16)],
        out_specs=[pl.BlockSpec((experts // 4, capacity, columns), lambda e: (e, 0, 0))],
        scratch=[pltpu.VMEM((group, columns), bf16)],
        grid=4,
        flops=DISPATCH_FLOPS,
    )
    sent, own_gain = lax.optimization_barrier((sent, own_gain))
    arrived = lax.all_to_all(sent, EXPERT, split_axis=0, concat_axis=2, tiled=True)

    d_gain = lax.psum(own_gain, "x")
    part = (features // xs // zl + PAD, columns)
    parts = call(
        low_split_kernel, lax.axis_index("zl").reshape(1), d_value, d_gain,
        out=[(part, bf16)] * zl, limit=8,
    )
    parts = [parts[0]] + [further(parts[k], "zl", k) for k in range(1, zl)]
    (parts,) = call(
        high_split_kernel, *parts, out=[((zh, rows + 8, columns), f32)], limit=8,
    )
    parts = lax.all_to_all(parts, "zh", 0, 0, tiled=True)
    d_value, d_gain = call(
        lambda *refs: finish_kernel(rescale, *refs), parts,
        out=[((rows, columns), bf16), ((1, columns), f32)], limit=8,
    )
    return (d_value, d_gain.reshape(columns), arrived)


def solution(mesh):
    split = Mesh(mesh.devices.reshape(4, 4, 4, 4, 2), ("zh", "zl", "x", "y", "core"))
    dp = ("zh", "zl", "x")
    return jax.shard_map(
        on_device,
        mesh=split,
        in_specs=(
            P(dp, EXPERT),
            P(dp + EXPERT, None),
            P(dp, EXPERT),
            P(EXPERT),
            P(dp, EXPERT),
            P(dp, None),
            P(dp, None),
        ),
        out_specs=(P(dp, EXPERT), P(EXPERT), P(EXPERT, dp, None)),
        check_vma=False,
    )
```

```python
import jax
import jax.numpy as jnp
from jax import lax
from jax.experimental import pallas as pl
from jax.experimental.pallas import tpu as pltpu
from jax.sharding import Mesh, PartitionSpec as P

epsilon = 1e-05
EXPERT = ("y", "core")
ANY = pl.BlockSpec(memory_space=pl.ANY)
HBM = pl.BlockSpec(memory_space=pltpu.HBM)
SMEM = pl.BlockSpec(memory_space=pltpu.SMEM)
PAD = 16
VALUE_LIMIT = 62
NORMED_LIMIT = 52
NORMED_FLOPS = 4 * 10**9
DISPATCH_FLOPS = 20 * 10**9


def whole(shape):
    return pl.BlockSpec(shape, lambda *at: (0,) * len(shape))


def call(
    kernel, *operands, out, limit=60, grid=1, scratch=(), in_specs=None, out_specs=None, flops=None
):
    cost = {}
    if flops:
        cost["cost_estimate"] = pl.CostEstimate(
            flops=flops, bytes_accessed=10**7, transcendentals=0
        )
    return pl.pallas_call(
        kernel,
        grid=(grid,),
        in_specs=in_specs or [SMEM if o.shape == (1,) else whole(o.shape) for o in operands],
        out_specs=out_specs or [whole(shape) for shape, _ in out],
        out_shape=[jax.ShapeDtypeStruct(shape, kind) for shape, kind in out],
        scratch_shapes=scratch,
        compiler_params=pltpu.CompilerParams(
            dimension_semantics=("arbitrary",), vmem_limit_bytes=limit * 2**20
        ),
        **cost,
    )(*operands)


def column(row):
    return jnp.transpose(jnp.broadcast_to(row, (8, row.shape[1])))[:, 0:1]


def pieces(row):
    high = row.astype(jnp.bfloat16).astype(jnp.float32)
    middle = (row - high).astype(jnp.bfloat16).astype(jnp.float32)
    low = row - high - middle
    at = lax.broadcasted_iota(jnp.int32, (PAD, row.shape[1]), 0)
    rows = jnp.where(at == 0, high, jnp.where(at == 1, middle, jnp.where(at == 2, low, 0.0)))
    return rows.astype(jnp.bfloat16)


def pack_kernel(value_ref, input_ref, weight_ref, packed_ref, copies_ref):
    rows = value_ref.shape[0]
    inputs = input_ref[...].astype(jnp.float32)
    squares = jnp.sum(inputs * inputs, axis=1, keepdims=True)
    row = jnp.transpose(jnp.broadcast_to(squares, (squares.shape[0], 8)))[0:1, :]
    packed_ref[0:rows, :] = value_ref[...]
    packed_ref[rows:, :] = pieces(row)
    for peer in range(copies_ref.shape[0]):
        copies_ref[peer] = weight_ref[...]


def route_kernel(routes_ref, logits_ref, slot_ref, gate_ref):
    experts, group = slot_ref.shape
    expert = lax.broadcasted_iota(jnp.int32, (experts, group), 0)
    first = routes_ref[0:1, :] == expert
    second = routes_ref[1:2, :] == expert
    named = jnp.where(first | second, 1.0, 0.0)
    earlier = lax.broadcasted_iota(jnp.int32, (group, group), 0) < lax.broadcasted_iota(
        jnp.int32, (group, group), 1
    )
    count = jnp.dot(
        named.astype(jnp.bfloat16),
        jnp.where(earlier, 1.0, 0.0).astype(jnp.bfloat16),
        preferred_element_type=jnp.float32,
    )
    slot_ref[...] = jnp.where(named > 0.0, count, -1.0).astype(jnp.int32)
    low, high = logits_ref[0:1, :], logits_ref[1:2, :]
    gate_first = 1.0 / (1.0 + jnp.exp(high - low))
    gate_second = 1.0 / (1.0 + jnp.exp(low - high))
    gate_ref[...] = jnp.where(first, gate_first, jnp.where(second, gate_second, 0.0))


def value_kernel(
    width, gathered_ref, whole_input_ref, gain_ref, d_value_ref, inverse_ref,
    squares_ref, input_ref, value_ref, normed_ref, partial_ref, sems,
):
    devices, rows, features = value_ref.shape
    group = input_ref.shape[0]
    get_squares = pltpu.make_async_copy(
        gathered_ref.at[:, pl.ds(rows, PAD), :], squares_ref, sems.at[0]
    )
    get_value = pltpu.make_async_copy(
        gathered_ref.at[:, pl.ds(0, rows), :], value_ref, sems.at[1]
    )
    get_input = pltpu.make_async_copy(whole_input_ref, input_ref, sems.at[2])
    get_squares.start()
    get_input.start()
    get_value.start()
    get_squares.wait()
    squares = jnp.zeros((1, group), jnp.float32)
    for device in range(devices):
        part = squares_ref[device].astype(jnp.float32)
        squares += jnp.sum(part, axis=0, keepdims=True)
    inverse = 1.0 / jnp.sqrt(squares / width + epsilon)
    tile = group // 8
    for at in range(8):
        inverse_ref[at : at + 1, :] = inverse[:, at * tile : (at + 1) * tile]
    get_input.wait()
    scaled = input_ref[...].astype(jnp.float32) * column(inverse)
    normed_ref[...] = (scaled * gain_ref[...]).astype(jnp.bfloat16)

    zh, xs, zl, own, _ = partial_ref.shape
    block = features // zh
    get_value.wait()
    puts = []
    for high in range(zh):
        partial = lax.dot_general(
            value_ref[:, :, high * block : (high + 1) * block].reshape(group, block),
            normed_ref[...],
            (((0,), (0,)), ((), ())),
            preferred_element_type=jnp.float32,
        )
        for low in range(zl):
            for x in range(xs):
                start = (low * xs + x) * own
                partial_ref[high, x, low] = partial[start : start + own, :]
        put = pltpu.make_async_copy(
            partial_ref.at[high], d_value_ref.at[:, :, high], sems.at[3 + high]
        )
        put.start()
        puts.append(put)
    for put in puts:
        put.wait()


def normed_kernel(
    me_ref, value_ref, input_ref, grad_ref, gain_ref, given_ref, *refs
):
    parts = refs[:-7]
    base_ref, inner_ref, d_gain_ref, inverse_ref, weight_ref, sems, sem = refs[-7:]
    step = pl.program_id(0)

    @pl.when(step == 0)
    def _():
        xs, zl = len(parts), parts[0].shape[0]
        gets = [pltpu.make_async_copy(given_ref, inverse_ref, sem)]
        gets[0].start()
        for x_step, part in enumerate(parts):
            x = lax.rem(me_ref[0] + (xs - x_step), xs)
            for low in range(zl):
                get = pltpu.make_async_copy(
                    part.at[low], weight_ref.at[:, low, x], sems.at[x_step, low]
                )
                get.start()
                gets.append(get)
        d_gain_ref[...] = jnp.zeros(d_gain_ref.shape, jnp.float32)
        for get in gets:
            get.wait()

    devices, rows, features = value_ref.shape
    d_normed = jnp.dot(
        value_ref[...].reshape(devices * rows, features),
        weight_ref[...].reshape(features, -1),
        preferred_element_type=jnp.float32,
    )
    d_gain = d_gain_ref[...]
    for at in range(devices):
        tokens = slice(at * rows, (at + 1) * rows)
        inverse = column(inverse_ref[pl.ds(step * devices + at, 1), :])
        normed = d_normed[tokens, :]
        scaled = input_ref[tokens, :].astype(jnp.float32) * inverse
        weighted = normed * gain_ref[...]
        d_gain += jnp.sum(normed * scaled, axis=0, keepdims=True)
        inner = jnp.sum(weighted * scaled, axis=1, keepdims=True)
        inner = jnp.transpose(jnp.broadcast_to(inner, (rows, 8)))[0:1, :]
        for peer in range(inner_ref.shape[0]):
            inner_ref[peer, pl.ds(step * devices + at, 1), :] = inner
        base_ref[tokens, :] = grad_ref[tokens, :].astype(jnp.float32) + weighted * inverse
    d_gain_ref[...] = d_gain


def dispatch_kernel(
    width, inverse_ref, inner_ref, slot_ref, gate_ref, base_ref, input_ref, out_ref, stream_ref
):
    step = pl.program_id(0)
    group = input_ref.shape[0]
    experts, capacity, _ = out_ref.shape

    @pl.when(step == 0)
    def _():
        inverse = inverse_ref[...]
        inner = jnp.sum(inner_ref[...], axis=0) / width
        factor = jnp.transpose(inner * inverse * inverse)
        tile = group // 8
        for at in range(8):
            rows = pl.ds(at * tile, tile)
            stream = (
                base_ref[rows, :]
                - input_ref[rows, :].astype(jnp.float32) * factor[:, at : at + 1]
            )
            stream_ref[rows, :] = stream.astype(jnp.bfloat16)

    for at in range(experts):
        slot = slot_ref[pl.ds(step * experts + at, 1), :]
        gate = gate_ref[pl.ds(step * experts + at, 1), :]
        taken = lax.broadcasted_iota(jnp.int32, (capacity, group), 0) == slot
        gates = jnp.sum(jnp.where(taken, gate, 0.0), axis=1, keepdims=True)
        picked = jnp.dot(
            jnp.where(taken, 1.0, 0.0).astype(jnp.bfloat16),
            stream_ref[...],
            preferred_element_type=jnp.float32,
        )
        out_ref[at] = (gates * picked).astype(jnp.bfloat16)


def low_split_kernel(me_ref, given_ref, d_gain_ref, *refs):
    outs, (d_value_ref, sem) = refs[:-2], refs[-2:]
    get = pltpu.make_async_copy(given_ref, d_value_ref, sem)
    get.start()
    get.wait()
    count = len(outs)
    rows = d_value_ref.shape[0] // count
    behind = pieces(d_gain_ref[...])
    for k, out in enumerate(outs):
        start = pl.multiple_of(lax.rem(me_ref[0] + k, count) * rows, rows)
        out[0:rows, :] = d_value_ref[pl.ds(start, rows), :].astype(jnp.bfloat16)
        out[rows:, :] = behind


def high_split_kernel(a_ref, b_ref, c_ref, d_ref, out_ref):
    total = a_ref[...].astype(jnp.float32)
    for ref in (b_ref, c_ref, d_ref):
        total += ref[...].astype(jnp.float32)
    count, own, _ = out_ref.shape
    columns = total.shape[1]
    rows = total.shape[0] - PAD
    gain = jnp.sum(total[rows:, :], axis=0, keepdims=True)
    parts = pieces(gain).astype(jnp.float32)
    blocks = columns // 128
    at = lax.broadcasted_iota(jnp.int32, (own, 128), 0)
    behind = jnp.zeros((own, 128), jnp.float32)
    for part in range(3):
        for block in range(blocks):
            row = parts[part : part + 1, block * 128 : (block + 1) * 128]
            behind = jnp.where(at == part * blocks + block, row, behind)
    for to in range(count):
        out_ref[to, :, 0:columns] = total[to * own : (to + 1) * own, :].astype(jnp.bfloat16)
        out_ref[to, :, columns:] = behind.astype(jnp.bfloat16)


def finish_kernel(rescale, parts_ref, d_value_ref, d_gain_ref):
    total = parts_ref[0].astype(jnp.float32)
    for at in range(1, parts_ref.shape[0]):
        total += parts_ref[at].astype(jnp.float32)
    columns = d_value_ref.shape[1]
    d_value_ref[...] = (total[:, 0:columns] * rescale).astype(jnp.bfloat16)
    blocks = columns // 128
    for block in range(blocks):
        gain = total[block : block + 1, columns:]
        for part in (1, 2):
            row = part * blocks + block
            gain += total[row : row + 1, columns:]
        d_gain_ref[:, block * 128 : (block + 1) * 128] = gain * rescale


def to_all(part, axis):
    size = lax.axis_size(axis)
    return lax.all_to_all(
        jnp.broadcast_to(part[None], (size,) + part.shape), axis, 0, 0, tiled=True
    )


def further(part, axis, step):
    size = lax.axis_size(axis)
    return lax.ppermute(part, axis, [(i, (i + step) % size) for i in range(size)])


def on_device(stream_grad, value_grad, attn_input, norm_gain, value_weight, gate_logits, routes):
    group, columns = attn_input.shape
    experts = lax.axis_size(EXPERT)
    zh, zl, xs = lax.axis_size("zh"), lax.axis_size("zl"), lax.axis_size("x")
    width = columns * experts
    tokens_all = group * zh * zl * xs
    rescale = float(tokens_all) ** (-0.5)
    capacity = min(group, 5 * group // (2 * experts))
    rows = value_weight.shape[0]
    features = rows * zh * zl * xs
    own_rows = value_grad.shape[0]
    f32, bf16 = jnp.float32, jnp.bfloat16
    gain_row = norm_gain[None]

    packed, copies = call(
        pack_kernel, value_grad, attn_input, value_weight,
        out=[((own_rows + PAD, features), bf16), ((zh, rows, columns), bf16)],
    )
    gathered = lax.all_gather(packed, EXPERT, axis=0)

    weight = to_all(lax.all_to_all(copies, "zh", 0, 0, tiled=True), "zl")
    weights = [weight] + [further(weight, "x", step) for step in range(1, xs)]
    gathered, weights[1] = lax.optimization_barrier((gathered, weights[1]))

    slot, gate = call(
        route_kernel, routes.T, gate_logits.T,
        out=[((experts, group), jnp.int32), ((experts, group), f32)],
    )

    d_value, inverse = call(
        lambda *refs: value_kernel(width, *refs), gathered, attn_input, gain_row,
        out=[((xs, zl, zh, rows, columns), f32), ((8, group // 8), f32)],
        in_specs=[ANY, ANY, whole((1, columns))],
        out_specs=[ANY, whole((8, group // 8))],
        scratch=[
            pltpu.VMEM((experts, PAD, features), bf16),
            pltpu.VMEM((group, columns), bf16),
            pltpu.VMEM((experts, own_rows, features), bf16),
            pltpu.VMEM((group, columns), bf16),
            pltpu.VMEM((zh, xs, zl, rows, columns), f32),
            pltpu.SemaphoreType.DMA((3 + zh,)),
        ],
        limit=VALUE_LIMIT,
    )
    d_value = lax.psum_scatter(
        d_value.reshape(features, columns), "x", scatter_dimension=0, tiled=True
    )

    half = pl.BlockSpec((group // 2, columns), lambda i: (i, 0))
    base, inner, own_gain = call(
        normed_kernel, lax.axis_index("x").reshape(1), gathered, attn_input, stream_grad,
        gain_row, inverse, *weights,
        out=[((group, columns), f32), ((experts, 8, group // 8), f32), ((1, columns), f32)],
        in_specs=[
            SMEM,
            pl.BlockSpec((experts // 2, own_rows, features), lambda i: (i, 0, 0)),
            half,
            half,
            whole((1, columns)),
            HBM,
        ]
        + [ANY] * xs,
        out_specs=[half, whole((experts, 8, group // 8)), whole((1, columns))],
        scratch=[
            pltpu.VMEM((8, group // 8), f32),
            pltpu.VMEM((zh, zl, xs, rows, columns), bf16),
            pltpu.SemaphoreType.DMA((xs, zl)),
            pltpu.SemaphoreType.DMA(()),
        ],
        grid=2,
        limit=NORMED_LIMIT,
        flops=NORMED_FLOPS,
    )
    inner = lax.all_to_all(inner, EXPERT, 0, 0, tiled=True)

    (sent,) = call(
        lambda *refs: dispatch_kernel(width, *refs),
        inverse, inner, slot, gate, base, attn_input,
        out=[((experts, capacity, columns), bf16)],
        out_specs=[pl.BlockSpec((experts // 4, capacity, columns), lambda e: (e, 0, 0))],
        scratch=[pltpu.VMEM((group, columns), bf16)],
        grid=4,
        flops=DISPATCH_FLOPS,
    )
    sent, own_gain = lax.optimization_barrier((sent, own_gain))
    arrived = lax.all_to_all(sent, EXPERT, split_axis=0, concat_axis=2, tiled=True)

    d_gain = lax.psum(own_gain, "x")
    part = (features // xs // zl + PAD, columns)
    parts = call(
        low_split_kernel, lax.axis_index("zl").reshape(1), d_value, d_gain,
        out=[(part, bf16)] * zl, limit=8,
        in_specs=[SMEM, HBM, whole((1, columns))],
        scratch=[pltpu.VMEM((features // xs, columns), f32), pltpu.SemaphoreType.DMA(())],
    )
    parts = [parts[0]] + [further(parts[k], "zl", k) for k in range(1, zl)]
    (parts,) = call(
        high_split_kernel, *parts, out=[((zh, rows, columns + 128), bf16)], limit=8,
    )
    parts = lax.all_to_all(parts, "zh", 0, 0, tiled=True)
    d_value, d_gain = call(
        lambda *refs: finish_kernel(rescale, *refs), parts,
        out=[((rows, columns), bf16), ((1, columns), f32)], limit=8,
    )
    return (d_value, d_gain.reshape(columns), arrived)


def solution(mesh):
    split = Mesh(mesh.devices.reshape(4, 4, 4, 4, 2), ("zh", "zl", "x", "y", "core"))
    dp = ("zh", "zl", "x")
    return jax.shard_map(
        on_device,
        mesh=split,
        in_specs=(
            P(dp, EXPERT),
            P(dp + EXPERT, None),
            P(dp, EXPERT),
            P(EXPERT),
            P(dp, EXPERT),
            P(dp, None),
            P(dp, None),
        ),
        out_specs=(P(dp, EXPERT), P(EXPERT), P(EXPERT, dp, None)),
        check_vma=False,
    )
```

```python
import jax
import jax.numpy as jnp
from jax import lax
from jax.experimental import pallas as pl
from jax.experimental.pallas import tpu as pltpu
from jax.sharding import Mesh, PartitionSpec as P

epsilon = 1e-05
EXPERT = ("y", "core")
ANY = pl.BlockSpec(memory_space=pl.ANY)
HBM = pl.BlockSpec(memory_space=pltpu.HBM)
SMEM = pl.BlockSpec(memory_space=pltpu.SMEM)
PAD = 16
VALUE_LIMIT = 62
NORMED_LIMIT = 52
DISPATCH_LIMIT = 52
NORMED_FLOPS = 4 * 10**9
DISPATCH_FLOPS = 20 * 10**9


def whole(shape):
    return pl.BlockSpec(shape, lambda *at: (0,) * len(shape))


def call(
    kernel, *operands, out, limit=60, grid=1, scratch=(), in_specs=None, out_specs=None, flops=None
):
    cost = {}
    if flops:
        cost["cost_estimate"] = pl.CostEstimate(
            flops=flops, bytes_accessed=10**7, transcendentals=0
        )
    return pl.pallas_call(
        kernel,
        grid=(grid,),
        in_specs=in_specs or [SMEM if o.shape == (1,) else whole(o.shape) for o in operands],
        out_specs=out_specs or [whole(shape) for shape, _ in out],
        out_shape=[jax.ShapeDtypeStruct(shape, kind) for shape, kind in out],
        scratch_shapes=scratch,
        compiler_params=pltpu.CompilerParams(
            dimension_semantics=("arbitrary",), vmem_limit_bytes=limit * 2**20
        ),
        **cost,
    )(*operands)


def column(row):
    return jnp.transpose(jnp.broadcast_to(row, (8, row.shape[1])))[:, 0:1]


def pieces(row):
    high = row.astype(jnp.bfloat16).astype(jnp.float32)
    middle = (row - high).astype(jnp.bfloat16).astype(jnp.float32)
    low = row - high - middle
    at = lax.broadcasted_iota(jnp.int32, (PAD, row.shape[1]), 0)
    rows = jnp.where(at == 0, high, jnp.where(at == 1, middle, jnp.where(at == 2, low, 0.0)))
    return rows.astype(jnp.bfloat16)


def pack_kernel(value_ref, input_ref, weight_ref, packed_ref, copies_ref):
    rows = value_ref.shape[0]
    inputs = input_ref[...].astype(jnp.float32)
    squares = jnp.sum(inputs * inputs, axis=1, keepdims=True)
    row = jnp.transpose(jnp.broadcast_to(squares, (squares.shape[0], 8)))[0:1, :]
    packed_ref[0:rows, :] = value_ref[...]
    packed_ref[rows:, :] = pieces(row)
    for peer in range(copies_ref.shape[0]):
        copies_ref[peer] = weight_ref[...]


def route_kernel(routes_ref, logits_ref, slot_ref, gate_ref):
    experts, group = slot_ref.shape
    expert = lax.broadcasted_iota(jnp.int32, (experts, group), 0)
    first = routes_ref[0:1, :] == expert
    second = routes_ref[1:2, :] == expert
    named = jnp.where(first | second, 1.0, 0.0)
    earlier = lax.broadcasted_iota(jnp.int32, (group, group), 0) < lax.broadcasted_iota(
        jnp.int32, (group, group), 1
    )
    count = jnp.dot(
        named.astype(jnp.bfloat16),
        jnp.where(earlier, 1.0, 0.0).astype(jnp.bfloat16),
        preferred_element_type=jnp.float32,
    )
    slot_ref[...] = jnp.where(named > 0.0, count, -1.0).astype(jnp.int32)
    low, high = logits_ref[0:1, :], logits_ref[1:2, :]
    gate_first = 1.0 / (1.0 + jnp.exp(high - low))
    gate_second = 1.0 / (1.0 + jnp.exp(low - high))
    gate_ref[...] = jnp.where(first, gate_first, jnp.where(second, gate_second, 0.0))


def value_kernel(
    width, gathered_ref, whole_input_ref, gain_ref, d_value_ref, inverse_ref,
    squares_ref, input_ref, value_ref, normed_ref, partial_ref, sems,
):
    devices, rows, features = value_ref.shape
    group = input_ref.shape[0]
    get_squares = pltpu.make_async_copy(
        gathered_ref.at[:, pl.ds(rows, PAD), :], squares_ref, sems.at[0]
    )
    get_value = pltpu.make_async_copy(
        gathered_ref.at[:, pl.ds(0, rows), :], value_ref, sems.at[1]
    )
    get_input = pltpu.make_async_copy(whole_input_ref, input_ref, sems.at[2])
    get_squares.start()
    get_input.start()
    get_value.start()
    get_squares.wait()
    squares = jnp.zeros((1, group), jnp.float32)
    for device in range(devices):
        part = squares_ref[device].astype(jnp.float32)
        squares += jnp.sum(part, axis=0, keepdims=True)
    inverse = 1.0 / jnp.sqrt(squares / width + epsilon)
    tile = group // 8
    for at in range(8):
        inverse_ref[at : at + 1, :] = inverse[:, at * tile : (at + 1) * tile]
    get_input.wait()
    scaled = input_ref[...].astype(jnp.float32) * column(inverse)
    normed_ref[...] = (scaled * gain_ref[...]).astype(jnp.bfloat16)

    zh, xs, zl, own, _ = partial_ref.shape
    block = features // zh
    get_value.wait()
    puts = []
    for high in range(zh):
        partial = lax.dot_general(
            value_ref[:, :, high * block : (high + 1) * block].reshape(group, block),
            normed_ref[...],
            (((0,), (0,)), ((), ())),
            preferred_element_type=jnp.float32,
        )
        for low in range(zl):
            for x in range(xs):
                start = (low * xs + x) * own
                partial_ref[high, x, low] = partial[start : start + own, :]
        put = pltpu.make_async_copy(
            partial_ref.at[high], d_value_ref.at[:, :, high], sems.at[3 + high]
        )
        put.start()
        puts.append(put)
    for put in puts:
        put.wait()


def normed_kernel(
    me_ref, value_ref, input_ref, grad_ref, gain_ref, given_ref, *refs
):
    parts = refs[:-7]
    base_ref, inner_ref, d_gain_ref, inverse_ref, weight_ref, sems, sem = refs[-7:]
    step = pl.program_id(0)

    @pl.when(step == 0)
    def _():
        xs, zl = len(parts), parts[0].shape[0]
        gets = [pltpu.make_async_copy(given_ref, inverse_ref, sem)]
        gets[0].start()
        for x_step, part in enumerate(parts):
            x = lax.rem(me_ref[0] + (xs - x_step), xs)
            for low in range(zl):
                get = pltpu.make_async_copy(
                    part.at[low], weight_ref.at[:, low, x], sems.at[x_step, low]
                )
                get.start()
                gets.append(get)
        d_gain_ref[...] = jnp.zeros(d_gain_ref.shape, jnp.float32)
        for get in gets:
            get.wait()

    devices, rows, features = value_ref.shape
    d_normed = jnp.dot(
        value_ref[...].reshape(devices * rows, features),
        weight_ref[...].reshape(features, -1),
        preferred_element_type=jnp.float32,
    )
    d_gain = d_gain_ref[...]
    for at in range(devices):
        tokens = slice(at * rows, (at + 1) * rows)
        inverse = column(inverse_ref[pl.ds(step * devices + at, 1), :])
        normed = d_normed[tokens, :]
        scaled = input_ref[tokens, :].astype(jnp.float32) * inverse
        weighted = normed * gain_ref[...]
        d_gain += jnp.sum(normed * scaled, axis=0, keepdims=True)
        inner = jnp.sum(weighted * scaled, axis=1, keepdims=True)
        inner = jnp.transpose(jnp.broadcast_to(inner, (rows, 8)))[0:1, :]
        for peer in range(inner_ref.shape[0]):
            inner_ref[peer, pl.ds(step * devices + at, 1), :] = inner
        base_ref[tokens, :] = grad_ref[tokens, :].astype(jnp.float32) + weighted * inverse
    d_gain_ref[...] = d_gain


def dispatch_kernel(
    width, inverse_ref, inner_ref, slot_ref, gate_ref, given_ref, input_ref, out_ref,
    base_ref, stream_ref, rows_ref, sems, get_sems,
):
    group = input_ref.shape[0]
    experts, capacity, _ = out_ref.shape
    quarter = group // 4
    gets = []
    for at in range(4):
        rows = pl.ds(at * quarter, quarter)
        get = pltpu.make_async_copy(given_ref.at[rows, :], base_ref.at[rows, :], get_sems.at[at])
        get.start()
        gets.append(get)
    inverse = inverse_ref[...]
    inner = jnp.sum(inner_ref[...], axis=0) / width
    factor = jnp.transpose(inner * inverse * inverse)
    tile = group // 8
    for at in range(8):
        rows = slice(at * tile, (at + 1) * tile)
        if at % 2 == 0:
            gets[at // 2].wait()
        stream = (
            base_ref[rows, :]
            - input_ref[rows, :].astype(jnp.float32) * factor[:, at : at + 1]
        )
        stream_ref[rows, :] = stream.astype(jnp.bfloat16)

    puts = []
    for expert in range(experts):
        slot = slot_ref[expert : expert + 1, :]
        gate = gate_ref[expert : expert + 1, :]
        taken = lax.broadcasted_iota(jnp.int32, (capacity, group), 0) == slot
        gates = jnp.sum(jnp.where(taken, gate, 0.0), axis=1, keepdims=True)
        picked = jnp.dot(
            jnp.where(taken, 1.0, 0.0).astype(jnp.bfloat16),
            stream_ref[...],
            preferred_element_type=jnp.float32,
        )
        rows_ref[expert] = (gates * picked).astype(jnp.bfloat16)
        put = pltpu.make_async_copy(rows_ref.at[expert], out_ref.at[expert], sems.at[expert])
        put.start()
        puts.append(put)
    for put in puts:
        put.wait()


def low_split_kernel(me_ref, given_ref, d_gain_ref, *refs):
    outs, (d_value_ref, sem) = refs[:-2], refs[-2:]
    get = pltpu.make_async_copy(given_ref, d_value_ref, sem)
    get.start()
    get.wait()
    count = len(outs)
    rows = d_value_ref.shape[0] // count
    behind = pieces(d_gain_ref[...])
    for k, out in enumerate(outs):
        start = pl.multiple_of(lax.rem(me_ref[0] + k, count) * rows, rows)
        out[0:rows, :] = d_value_ref[pl.ds(start, rows), :].astype(jnp.bfloat16)
        out[rows:, :] = behind


def high_split_kernel(a_ref, b_ref, c_ref, d_ref, out_ref):
    total = a_ref[...].astype(jnp.float32)
    for ref in (b_ref, c_ref, d_ref):
        total += ref[...].astype(jnp.float32)
    count, own, _ = out_ref.shape
    columns = total.shape[1]
    rows = total.shape[0] - PAD
    gain = jnp.sum(total[rows:, :], axis=0, keepdims=True)
    parts = pieces(gain).astype(jnp.float32)
    blocks = columns // 128
    at = lax.broadcasted_iota(jnp.int32, (own, 128), 0)
    behind = jnp.zeros((own, 128), jnp.float32)
    for part in range(3):
        for block in range(blocks):
            row = parts[part : part + 1, block * 128 : (block + 1) * 128]
            behind = jnp.where(at == part * blocks + block, row, behind)
    for to in range(count):
        out_ref[to, :, 0:columns] = total[to * own : (to + 1) * own, :].astype(jnp.bfloat16)
        out_ref[to, :, columns:] = behind.astype(jnp.bfloat16)


def finish_kernel(rescale, parts_ref, d_value_ref, d_gain_ref):
    total = parts_ref[0].astype(jnp.float32)
    for at in range(1, parts_ref.shape[0]):
        total += parts_ref[at].astype(jnp.float32)
    columns = d_value_ref.shape[1]
    d_value_ref[...] = (total[:, 0:columns] * rescale).astype(jnp.bfloat16)
    blocks = columns // 128
    for block in range(blocks):
        gain = total[block : block + 1, columns:]
        for part in (1, 2):
            row = part * blocks + block
            gain += total[row : row + 1, columns:]
        d_gain_ref[:, block * 128 : (block + 1) * 128] = gain * rescale


def to_all(part, axis):
    size = lax.axis_size(axis)
    return lax.all_to_all(
        jnp.broadcast_to(part[None], (size,) + part.shape), axis, 0, 0, tiled=True
    )


def further(part, axis, step):
    size = lax.axis_size(axis)
    return lax.ppermute(part, axis, [(i, (i + step) % size) for i in range(size)])


def on_device(stream_grad, value_grad, attn_input, norm_gain, value_weight, gate_logits, routes):
    group, columns = attn_input.shape
    experts = lax.axis_size(EXPERT)
    zh, zl, xs = lax.axis_size("zh"), lax.axis_size("zl"), lax.axis_size("x")
    width = columns * experts
    tokens_all = group * zh * zl * xs
    rescale = float(tokens_all) ** (-0.5)
    capacity = min(group, 5 * group // (2 * experts))
    rows = value_weight.shape[0]
    features = rows * zh * zl * xs
    own_rows = value_grad.shape[0]
    f32, bf16 = jnp.float32, jnp.bfloat16
    gain_row = norm_gain[None]

    packed, copies = call(
        pack_kernel, value_grad, attn_input, value_weight,
        out=[((own_rows + PAD, features), bf16), ((zh, rows, columns), bf16)],
    )
    gathered = lax.all_gather(packed, EXPERT, axis=0)

    weight = to_all(lax.all_to_all(copies, "zh", 0, 0, tiled=True), "zl")
    weights = [weight] + [further(weight, "x", step) for step in range(1, xs)]
    gathered, weights[1] = lax.optimization_barrier((gathered, weights[1]))

    slot, gate = call(
        route_kernel, routes.T, gate_logits.T,
        out=[((experts, group), jnp.int32), ((experts, group), f32)],
        limit=24,
    )

    d_value, inverse = call(
        lambda *refs: value_kernel(width, *refs), gathered, attn_input, gain_row,
        out=[((xs, zl, zh, rows, columns), f32), ((8, group // 8), f32)],
        in_specs=[ANY, ANY, whole((1, columns))],
        out_specs=[ANY, whole((8, group // 8))],
        scratch=[
            pltpu.VMEM((experts, PAD, features), bf16),
            pltpu.VMEM((group, columns), bf16),
            pltpu.VMEM((experts, own_rows, features), bf16),
            pltpu.VMEM((group, columns), bf16),
            pltpu.VMEM((zh, xs, zl, rows, columns), f32),
            pltpu.SemaphoreType.DMA((3 + zh,)),
        ],
        limit=VALUE_LIMIT,
    )
    d_value = lax.psum_scatter(
        d_value.reshape(features, columns), "x", scatter_dimension=0, tiled=True
    )

    half = pl.BlockSpec((group // 2, columns), lambda i: (i, 0))
    base, inner, own_gain = call(
        normed_kernel, lax.axis_index("x").reshape(1), gathered, attn_input, stream_grad,
        gain_row, inverse, *weights,
        out=[((group, columns), f32), ((experts, 8, group // 8), f32), ((1, columns), f32)],
        in_specs=[
            SMEM,
            pl.BlockSpec((experts // 2, own_rows, features), lambda i: (i, 0, 0)),
            half,
            half,
            whole((1, columns)),
            HBM,
        ]
        + [ANY] * xs,
        out_specs=[half, whole((experts, 8, group // 8)), whole((1, columns))],
        scratch=[
            pltpu.VMEM((8, group // 8), f32),
            pltpu.VMEM((zh, zl, xs, rows, columns), bf16),
            pltpu.SemaphoreType.DMA((xs, zl)),
            pltpu.SemaphoreType.DMA(()),
        ],
        grid=2,
        limit=NORMED_LIMIT,
        flops=NORMED_FLOPS,
    )
    inner = lax.all_to_all(inner, EXPERT, 0, 0, tiled=True)

    (sent,) = call(
        lambda *refs: dispatch_kernel(width, *refs),
        inverse, inner, slot, gate, base, attn_input,
        out=[((experts, capacity, columns), bf16)],
        in_specs=[
            whole((8, group // 8)),
            whole((experts, 8, group // 8)),
            whole((experts, group)),
            whole((experts, group)),
            ANY,
            whole((group, columns)),
        ],
        out_specs=[ANY],
        scratch=[
            pltpu.VMEM((group, columns), f32),
            pltpu.VMEM((group, columns), bf16),
            pltpu.VMEM((experts, capacity, columns), bf16),
            pltpu.SemaphoreType.DMA((experts,)),
            pltpu.SemaphoreType.DMA((4,)),
        ],
        limit=DISPATCH_LIMIT,
        flops=DISPATCH_FLOPS,
    )
    sent, own_gain = lax.optimization_barrier((sent, own_gain))
    arrived = lax.all_to_all(sent, EXPERT, split_axis=0, concat_axis=2, tiled=True)

    d_gain = lax.psum(own_gain, "x")
    part = (features // xs // zl + PAD, columns)
    parts = call(
        low_split_kernel, lax.axis_index("zl").reshape(1), d_value, d_gain,
        out=[(part, bf16)] * zl, limit=8,
        in_specs=[SMEM, HBM, whole((1, columns))],
        scratch=[pltpu.VMEM((features // xs, columns), f32), pltpu.SemaphoreType.DMA(())],
    )
    parts = [parts[0]] + [further(parts[k], "zl", k) for k in range(1, zl)]
    (parts,) = call(
        high_split_kernel, *parts, out=[((zh, rows, columns + 128), bf16)], limit=8,
    )
    parts = lax.all_to_all(parts, "zh", 0, 0, tiled=True)
    d_value, d_gain = call(
        lambda *refs: finish_kernel(rescale, *refs), parts,
        out=[((rows, columns), bf16), ((1, columns), f32)], limit=8,
    )
    return (d_value, d_gain.reshape(columns), arrived)


def solution(mesh):
    split = Mesh(mesh.devices.reshape(4, 4, 4, 4, 2), ("zh", "zl", "x", "y", "core"))
    dp = ("zh", "zl", "x")
    return jax.shard_map(
        on_device,
        mesh=split,
        in_specs=(
            P(dp, EXPERT),
            P(dp + EXPERT, None),
            P(dp, EXPERT),
            P(EXPERT),
            P(dp, EXPERT),
            P(dp, None),
            P(dp, None),
        ),
        out_specs=(P(dp, EXPERT), P(EXPERT), P(EXPERT, dp, None)),
        check_vma=False,
    )
```

```python
import jax
import jax.numpy as jnp
from jax import lax
from jax.experimental import pallas as pl
from jax.experimental.pallas import tpu as pltpu
from jax.sharding import Mesh, PartitionSpec as P

epsilon = 1e-05
EXPERT = ("y", "core")
ANY = pl.BlockSpec(memory_space=pl.ANY)
HBM = pl.BlockSpec(memory_space=pltpu.HBM)
SMEM = pl.BlockSpec(memory_space=pltpu.SMEM)
PAD = 16
VALUE_LIMIT = 62
NORMED_LIMIT = 52
DISPATCH_LIMIT = 52
NORMED_FLOPS = 4 * 10**9
DISPATCH_FLOPS = 20 * 10**9


def whole(shape):
    return pl.BlockSpec(shape, lambda *at: (0,) * len(shape))


def call(
    kernel, *operands, out, limit=60, grid=1, scratch=(), in_specs=None, out_specs=None, flops=None
):
    cost = {}
    if flops:
        cost["cost_estimate"] = pl.CostEstimate(
            flops=flops, bytes_accessed=10**7, transcendentals=0
        )
    return pl.pallas_call(
        kernel,
        grid=(grid,),
        in_specs=in_specs or [SMEM if o.shape == (1,) else whole(o.shape) for o in operands],
        out_specs=out_specs or [whole(shape) for shape, _ in out],
        out_shape=[jax.ShapeDtypeStruct(shape, kind) for shape, kind in out],
        scratch_shapes=scratch,
        compiler_params=pltpu.CompilerParams(
            dimension_semantics=("arbitrary",), vmem_limit_bytes=limit * 2**20
        ),
        **cost,
    )(*operands)


def column(row):
    return jnp.transpose(jnp.broadcast_to(row, (8, row.shape[1])))[:, 0:1]


def pieces(row):
    high = row.astype(jnp.bfloat16).astype(jnp.float32)
    middle = (row - high).astype(jnp.bfloat16).astype(jnp.float32)
    low = row - high - middle
    at = lax.broadcasted_iota(jnp.int32, (PAD, row.shape[1]), 0)
    rows = jnp.where(at == 0, high, jnp.where(at == 1, middle, jnp.where(at == 2, low, 0.0)))
    return rows.astype(jnp.bfloat16)


def pack_kernel(value_ref, input_ref, weight_ref, packed_ref, copies_ref):
    rows = value_ref.shape[0]
    inputs = input_ref[...].astype(jnp.float32)
    squares = jnp.sum(inputs * inputs, axis=1, keepdims=True)
    row = jnp.transpose(jnp.broadcast_to(squares, (squares.shape[0], 8)))[0:1, :]
    packed_ref[0:rows, :] = value_ref[...]
    packed_ref[rows:, :] = pieces(row)
    for peer in range(copies_ref.shape[0]):
        copies_ref[peer] = weight_ref[...]


def route_kernel(routes_ref, logits_ref, slot_ref, gate_ref):
    experts, group = slot_ref.shape
    expert = lax.broadcasted_iota(jnp.int32, (experts, group), 0)
    first = routes_ref[0:1, :] == expert
    second = routes_ref[1:2, :] == expert
    named = jnp.where(first | second, 1.0, 0.0)
    earlier = lax.broadcasted_iota(jnp.int32, (group, group), 0) < lax.broadcasted_iota(
        jnp.int32, (group, group), 1
    )
    count = jnp.dot(
        named.astype(jnp.bfloat16),
        jnp.where(earlier, 1.0, 0.0).astype(jnp.bfloat16),
        preferred_element_type=jnp.float32,
    )
    slot_ref[...] = jnp.where(named > 0.0, count, -1.0).astype(jnp.int32)
    low, high = logits_ref[0:1, :], logits_ref[1:2, :]
    gate_first = 1.0 / (1.0 + jnp.exp(high - low))
    gate_second = 1.0 / (1.0 + jnp.exp(low - high))
    gate_ref[...] = jnp.where(first, gate_first, jnp.where(second, gate_second, 0.0))


def value_kernel(
    width, gathered_ref, whole_input_ref, gain_ref, d_value_ref, inverse_ref,
    squares_ref, input_ref, value_ref, normed_ref, partial_ref, sems,
):
    devices, rows, features = value_ref.shape
    group = input_ref.shape[0]
    get_squares = pltpu.make_async_copy(
        gathered_ref.at[:, pl.ds(rows, PAD), :], squares_ref, sems.at[0]
    )
    get_value = pltpu.make_async_copy(
        gathered_ref.at[:, pl.ds(0, rows), :], value_ref, sems.at[1]
    )
    get_input = pltpu.make_async_copy(whole_input_ref, input_ref, sems.at[2])
    get_squares.start()
    get_input.start()
    get_value.start()
    get_squares.wait()
    squares = jnp.zeros((1, group), jnp.float32)
    for device in range(devices):
        part = squares_ref[device].astype(jnp.float32)
        squares += jnp.sum(part, axis=0, keepdims=True)
    inverse = 1.0 / jnp.sqrt(squares / width + epsilon)
    tile = group // 8
    for at in range(8):
        inverse_ref[at : at + 1, :] = inverse[:, at * tile : (at + 1) * tile]
    get_input.wait()
    scaled = input_ref[...].astype(jnp.float32) * column(inverse)
    normed_ref[...] = (scaled * gain_ref[...]).astype(jnp.bfloat16)

    zh, xs, zl, own, _ = partial_ref.shape
    block = features // zh
    get_value.wait()
    puts = []
    for high in range(zh):
        partial = lax.dot_general(
            value_ref[:, :, high * block : (high + 1) * block].reshape(group, block),
            normed_ref[...],
            (((0,), (0,)), ((), ())),
            preferred_element_type=jnp.float32,
        )
        for low in range(zl):
            for x in range(xs):
                start = (low * xs + x) * own
                partial_ref[high, x, low] = partial[start : start + own, :]
        put = pltpu.make_async_copy(
            partial_ref.at[high], d_value_ref.at[:, :, high], sems.at[3 + high]
        )
        put.start()
        puts.append(put)
    for put in puts:
        put.wait()


def normed_kernel(
    me_ref, value_ref, input_ref, grad_ref, gain_ref, given_ref, *refs
):
    parts = refs[:-7]
    base_ref, inner_ref, d_gain_ref, inverse_ref, weight_ref, sems, sem = refs[-7:]
    step = pl.program_id(0)

    @pl.when(step == 0)
    def _():
        xs = len(parts)
        gets = [pltpu.make_async_copy(given_ref, inverse_ref, sem)]
        gets[0].start()
        for x_step, part in enumerate(parts):
            x = lax.rem(me_ref[0] + (xs - x_step), xs)
            get = pltpu.make_async_copy(part, weight_ref.at[:, :, x], sems.at[x_step])
            get.start()
            gets.append(get)
        d_gain_ref[...] = jnp.zeros(d_gain_ref.shape, jnp.float32)
        for get in gets:
            get.wait()

    devices, rows, features = value_ref.shape
    d_normed = jnp.dot(
        value_ref[...].reshape(devices * rows, features),
        weight_ref[...].reshape(features, -1),
        preferred_element_type=jnp.float32,
    )
    d_gain = d_gain_ref[...]
    for at in range(devices):
        tokens = slice(at * rows, (at + 1) * rows)
        inverse = column(inverse_ref[pl.ds(step * devices + at, 1), :])
        normed = d_normed[tokens, :]
        scaled = input_ref[tokens, :].astype(jnp.float32) * inverse
        weighted = normed * gain_ref[...]
        d_gain += jnp.sum(normed * scaled, axis=0, keepdims=True)
        inner = jnp.sum(weighted * scaled, axis=1, keepdims=True)
        inner = jnp.transpose(jnp.broadcast_to(inner, (rows, 8)))[0:1, :]
        for peer in range(inner_ref.shape[0]):
            inner_ref[peer, pl.ds(step * devices + at, 1), :] = inner
        base_ref[tokens, :] = grad_ref[tokens, :].astype(jnp.float32) + weighted * inverse
    d_gain_ref[...] = d_gain


def dispatch_kernel(
    width, inverse_ref, inner_ref, slot_ref, gate_ref, given_ref, input_ref, out_ref,
    base_ref, stream_ref, rows_ref, sems, get_sems,
):
    group = input_ref.shape[0]
    experts, capacity, _ = out_ref.shape
    quarter = group // 4
    gets = []
    for at in range(4):
        rows = pl.ds(at * quarter, quarter)
        get = pltpu.make_async_copy(given_ref.at[rows, :], base_ref.at[rows, :], get_sems.at[at])
        get.start()
        gets.append(get)
    inverse = inverse_ref[...]
    inner = jnp.sum(inner_ref[...], axis=0) / width
    factor = jnp.transpose(inner * inverse * inverse)
    tile = group // 8
    for at in range(8):
        rows = slice(at * tile, (at + 1) * tile)
        if at % 2 == 0:
            gets[at // 2].wait()
        stream = (
            base_ref[rows, :]
            - input_ref[rows, :].astype(jnp.float32) * factor[:, at : at + 1]
        )
        stream_ref[rows, :] = stream.astype(jnp.bfloat16)

    puts = []
    for expert in range(experts):
        slot = slot_ref[expert : expert + 1, :]
        gate = gate_ref[expert : expert + 1, :]
        taken = lax.broadcasted_iota(jnp.int32, (capacity, group), 0) == slot
        gates = jnp.sum(jnp.where(taken, gate, 0.0), axis=1, keepdims=True)
        picked = jnp.dot(
            jnp.where(taken, 1.0, 0.0).astype(jnp.bfloat16),
            stream_ref[...],
            preferred_element_type=jnp.float32,
        )
        rows_ref[expert] = (gates * picked).astype(jnp.bfloat16)
        put = pltpu.make_async_copy(rows_ref.at[expert], out_ref.at[expert], sems.at[expert])
        put.start()
        puts.append(put)
    for put in puts:
        put.wait()


def low_split_kernel(me_ref, given_ref, d_gain_ref, *refs):
    outs, (d_value_ref, sem) = refs[:-2], refs[-2:]
    get = pltpu.make_async_copy(given_ref, d_value_ref, sem)
    get.start()
    get.wait()
    count = len(outs)
    rows = d_value_ref.shape[0] // count
    behind = pieces(d_gain_ref[...])
    for k, out in enumerate(outs):
        start = pl.multiple_of(lax.rem(me_ref[0] + k, count) * rows, rows)
        out[0:rows, :] = d_value_ref[pl.ds(start, rows), :].astype(jnp.bfloat16)
        out[rows:, :] = behind


def high_split_kernel(a_ref, b_ref, c_ref, d_ref, out_ref):
    total = a_ref[...].astype(jnp.float32)
    for ref in (b_ref, c_ref, d_ref):
        total += ref[...].astype(jnp.float32)
    count, own, _ = out_ref.shape
    columns = total.shape[1]
    rows = total.shape[0] - PAD
    gain = jnp.sum(total[rows:, :], axis=0, keepdims=True)
    parts = pieces(gain).astype(jnp.float32)
    blocks = columns // 128
    at = lax.broadcasted_iota(jnp.int32, (own, 128), 0)
    behind = jnp.zeros((own, 128), jnp.float32)
    for part in range(3):
        for block in range(blocks):
            row = parts[part : part + 1, block * 128 : (block + 1) * 128]
            behind = jnp.where(at == part * blocks + block, row, behind)
    for to in range(count):
        out_ref[to, :, 0:columns] = total[to * own : (to + 1) * own, :].astype(jnp.bfloat16)
        out_ref[to, :, columns:] = behind.astype(jnp.bfloat16)


def finish_kernel(rescale, parts_ref, d_value_ref, d_gain_ref):
    total = parts_ref[0].astype(jnp.float32)
    for at in range(1, parts_ref.shape[0]):
        total += parts_ref[at].astype(jnp.float32)
    columns = d_value_ref.shape[1]
    d_value_ref[...] = (total[:, 0:columns] * rescale).astype(jnp.bfloat16)
    blocks = columns // 128
    for block in range(blocks):
        gain = total[block : block + 1, columns:]
        for part in (1, 2):
            row = part * blocks + block
            gain += total[row : row + 1, columns:]
        d_gain_ref[:, block * 128 : (block + 1) * 128] = gain * rescale


def to_all(part, axis):
    size = lax.axis_size(axis)
    return lax.all_to_all(
        jnp.broadcast_to(part[None], (size,) + part.shape), axis, 0, 0, tiled=True
    )


def further(part, axis, step):
    size = lax.axis_size(axis)
    return lax.ppermute(part, axis, [(i, (i + step) % size) for i in range(size)])


def on_device(stream_grad, value_grad, attn_input, norm_gain, value_weight, gate_logits, routes):
    group, columns = attn_input.shape
    experts = lax.axis_size(EXPERT)
    zh, zl, xs = lax.axis_size("zh"), lax.axis_size("zl"), lax.axis_size("x")
    width = columns * experts
    tokens_all = group * zh * zl * xs
    rescale = float(tokens_all) ** (-0.5)
    capacity = min(group, 5 * group // (2 * experts))
    rows = value_weight.shape[0]
    features = rows * zh * zl * xs
    own_rows = value_grad.shape[0]
    f32, bf16 = jnp.float32, jnp.bfloat16
    gain_row = norm_gain[None]

    packed, copies = call(
        pack_kernel, value_grad, attn_input, value_weight,
        out=[((own_rows + PAD, features), bf16), ((zh * zl, rows, columns), bf16)],
    )
    gathered = lax.all_gather(packed, EXPERT, axis=0)

    weight = lax.all_to_all(copies, ("zh", "zl"), 0, 0, tiled=True)
    weight = weight.reshape(zh, zl, rows, columns)
    weights = [weight] + [further(weight, "x", step) for step in range(1, xs)]
    gathered, weights[1] = lax.optimization_barrier((gathered, weights[1]))

    slot, gate = call(
        route_kernel, routes.T, gate_logits.T,
        out=[((experts, group), jnp.int32), ((experts, group), f32)],
        limit=24,
    )

    d_value, inverse = call(
        lambda *refs: value_kernel(width, *refs), gathered, attn_input, gain_row,
        out=[((xs, zl, zh, rows, columns), f32), ((8, group // 8), f32)],
        in_specs=[ANY, ANY, whole((1, columns))],
        out_specs=[ANY, whole((8, group // 8))],
        scratch=[
            pltpu.VMEM((experts, PAD, features), bf16),
            pltpu.VMEM((group, columns), bf16),
            pltpu.VMEM((experts, own_rows, features), bf16),
            pltpu.VMEM((group, columns), bf16),
            pltpu.VMEM((zh, xs, zl, rows, columns), f32),
            pltpu.SemaphoreType.DMA((3 + zh,)),
        ],
        limit=VALUE_LIMIT,
    )
    d_value = lax.psum_scatter(
        d_value.reshape(features, columns), "x", scatter_dimension=0, tiled=True
    )

    half = pl.BlockSpec((group // 2, columns), lambda i: (i, 0))
    base, inner, own_gain = call(
        normed_kernel, lax.axis_index("x").reshape(1), gathered, attn_input, stream_grad,
        gain_row, inverse, *weights,
        out=[((group, columns), f32), ((experts, 8, group // 8), f32), ((1, columns), f32)],
        in_specs=[
            SMEM,
            pl.BlockSpec((experts // 2, own_rows, features), lambda i: (i, 0, 0)),
            half,
            half,
            whole((1, columns)),
            HBM,
        ]
        + [ANY] * xs,
        out_specs=[half, whole((experts, 8, group // 8)), whole((1, columns))],
        scratch=[
            pltpu.VMEM((8, group // 8), f32),
            pltpu.VMEM((zh, zl, xs, rows, columns), bf16),
            pltpu.SemaphoreType.DMA((xs,)),
            pltpu.SemaphoreType.DMA(()),
        ],
        grid=2,
        limit=NORMED_LIMIT,
        flops=NORMED_FLOPS,
    )
    inner = lax.all_to_all(inner, EXPERT, 0, 0, tiled=True)

    (sent,) = call(
        lambda *refs: dispatch_kernel(width, *refs),
        inverse, inner, slot, gate, base, attn_input,
        out=[((experts, capacity, columns), bf16)],
        in_specs=[
            whole((8, group // 8)),
            whole((experts, 8, group // 8)),
            whole((experts, group)),
            whole((experts, group)),
            ANY,
            whole((group, columns)),
        ],
        out_specs=[ANY],
        scratch=[
            pltpu.VMEM((group, columns), f32),
            pltpu.VMEM((group, columns), bf16),
            pltpu.VMEM((experts, capacity, columns), bf16),
            pltpu.SemaphoreType.DMA((experts,)),
            pltpu.SemaphoreType.DMA((4,)),
        ],
        limit=DISPATCH_LIMIT,
        flops=DISPATCH_FLOPS,
    )
    sent, own_gain = lax.optimization_barrier((sent, own_gain))
    arrived = lax.all_to_all(sent, EXPERT, split_axis=0, concat_axis=2, tiled=True)

    d_gain = lax.psum(own_gain, "x")
    part = (features // xs // zl + PAD, columns)
    parts = call(
        low_split_kernel, lax.axis_index("zl").reshape(1), d_value, d_gain,
        out=[(part, bf16)] * zl, limit=8,
        in_specs=[SMEM, HBM, whole((1, columns))],
        scratch=[pltpu.VMEM((features // xs, columns), f32), pltpu.SemaphoreType.DMA(())],
    )
    parts = [parts[0]] + [further(parts[k], "zl", k) for k in range(1, zl)]
    (parts,) = call(
        high_split_kernel, *parts, out=[((zh, rows, columns + 128), bf16)], limit=8,
    )
    parts = lax.all_to_all(parts, "zh", 0, 0, tiled=True)
    d_value, d_gain = call(
        lambda *refs: finish_kernel(rescale, *refs), parts,
        out=[((rows, columns), bf16), ((1, columns), f32)], limit=8,
    )
    return (d_value, d_gain.reshape(columns), arrived)


def solution(mesh):
    split = Mesh(mesh.devices.reshape(4, 4, 4, 4, 2), ("zh", "zl", "x", "y", "core"))
    dp = ("zh", "zl", "x")
    return jax.shard_map(
        on_device,
        mesh=split,
        in_specs=(
            P(dp, EXPERT),
            P(dp + EXPERT, None),
            P(dp, EXPERT),
            P(EXPERT),
            P(dp, EXPERT),
            P(dp, None),
            P(dp, None),
        ),
        out_specs=(P(dp, EXPERT), P(EXPERT), P(EXPERT, dp, None)),
        check_vma=False,
    )
```

```python
import jax
import jax.numpy as jnp
from jax import lax
from jax.experimental import pallas as pl
from jax.experimental.pallas import tpu as pltpu
from jax.sharding import Mesh, PartitionSpec as P

epsilon = 1e-05
EXPERT = ("y", "core")
ANY = pl.BlockSpec(memory_space=pl.ANY)
HBM = pl.BlockSpec(memory_space=pltpu.HBM)
SMEM = pl.BlockSpec(memory_space=pltpu.SMEM)
PAD = 16
VALUE_LIMIT = 62
NORMED_LIMIT = 52
DISPATCH_LIMIT = 52
NORMED_FLOPS = 4 * 10**9
DISPATCH_FLOPS = 20 * 10**9


def whole(shape):
    return pl.BlockSpec(shape, lambda *at: (0,) * len(shape))


def call(
    kernel, *operands, out, limit=60, grid=1, scratch=(), in_specs=None, out_specs=None, flops=None
):
    cost = {}
    if flops:
        cost["cost_estimate"] = pl.CostEstimate(
            flops=flops, bytes_accessed=10**7, transcendentals=0
        )
    return pl.pallas_call(
        kernel,
        grid=(grid,),
        in_specs=in_specs or [SMEM if o.shape == (1,) else whole(o.shape) for o in operands],
        out_specs=out_specs or [whole(shape) for shape, _ in out],
        out_shape=[jax.ShapeDtypeStruct(shape, kind) for shape, kind in out],
        scratch_shapes=scratch,
        compiler_params=pltpu.CompilerParams(
            dimension_semantics=("arbitrary",), vmem_limit_bytes=limit * 2**20
        ),
        **cost,
    )(*operands)


def column(row):
    return jnp.transpose(jnp.broadcast_to(row, (8, row.shape[1])))[:, 0:1]


def pieces(row):
    high = row.astype(jnp.bfloat16).astype(jnp.float32)
    middle = (row - high).astype(jnp.bfloat16).astype(jnp.float32)
    low = row - high - middle
    at = lax.broadcasted_iota(jnp.int32, (PAD, row.shape[1]), 0)
    rows = jnp.where(at == 0, high, jnp.where(at == 1, middle, jnp.where(at == 2, low, 0.0)))
    return rows.astype(jnp.bfloat16)


def squares_kernel(input_ref, squares_ref):
    tile = squares_ref.shape[1]
    for at in range(squares_ref.shape[0]):
        inputs = input_ref[at * tile : (at + 1) * tile, :].astype(jnp.float32)
        squares = jnp.sum(inputs * inputs, axis=1, keepdims=True)
        squares_ref[at : at + 1, :] = jnp.transpose(jnp.broadcast_to(squares, (tile, 8)))[0:1, :]


def norm_kernel(width, squares_ref, input_ref, gain_ref, normed_ref, inverse_ref):
    inverse = 1.0 / jnp.sqrt(squares_ref[...] / width + epsilon)
    inverse_ref[...] = inverse
    factor = jnp.transpose(inverse)
    tile = inverse.shape[1]
    for at in range(inverse.shape[0]):
        tokens = slice(at * tile, (at + 1) * tile)
        scaled = input_ref[tokens, :].astype(jnp.float32) * factor[:, at : at + 1]
        normed_ref[tokens, :] = (scaled * gain_ref[...]).astype(jnp.bfloat16)


def route_kernel(routes_ref, logits_ref, slot_ref, gate_ref):
    experts, group = slot_ref.shape
    expert = lax.broadcasted_iota(jnp.int32, (experts, group), 0)
    first = routes_ref[0:1, :] == expert
    second = routes_ref[1:2, :] == expert
    named = jnp.where(first | second, 1.0, 0.0)
    earlier = lax.broadcasted_iota(jnp.int32, (group, group), 0) < lax.broadcasted_iota(
        jnp.int32, (group, group), 1
    )
    count = jnp.dot(
        named.astype(jnp.bfloat16),
        jnp.where(earlier, 1.0, 0.0).astype(jnp.bfloat16),
        preferred_element_type=jnp.float32,
    )
    slot_ref[...] = jnp.where(named > 0.0, count, -1.0).astype(jnp.int32)
    low, high = logits_ref[0:1, :], logits_ref[1:2, :]
    gate_first = 1.0 / (1.0 + jnp.exp(high - low))
    gate_second = 1.0 / (1.0 + jnp.exp(low - high))
    gate_ref[...] = jnp.where(first, gate_first, jnp.where(second, gate_second, 0.0))


def value_kernel(given_ref, normed_ref, d_value_ref, value_ref, partial_ref, get_sem, sems):
    get = pltpu.make_async_copy(given_ref, value_ref, get_sem)
    get.start()
    zh, xs, zl, own, _ = partial_ref.shape
    group = normed_ref.shape[0]
    block = value_ref.shape[2] // zh
    get.wait()
    puts = []
    for high in range(zh):
        partial = lax.dot_general(
            value_ref[:, :, high * block : (high + 1) * block].reshape(group, block),
            normed_ref[...],
            (((0,), (0,)), ((), ())),
            preferred_element_type=jnp.float32,
        )
        for low in range(zl):
            for x in range(xs):
                start = (low * xs + x) * own
                partial_ref[high, x, low] = partial[start : start + own, :]
        put = pltpu.make_async_copy(
            partial_ref.at[high], d_value_ref.at[:, :, high], sems.at[high]
        )
        put.start()
        puts.append(put)
    for put in puts:
        put.wait()


def normed_kernel(
    me_ref, value_ref, input_ref, grad_ref, gain_ref, given_ref, *refs
):
    parts = refs[:-7]
    base_ref, inner_ref, d_gain_ref, inverse_ref, weight_ref, sems, sem = refs[-7:]
    step = pl.program_id(0)

    @pl.when(step == 0)
    def _():
        xs = len(parts)
        gets = [pltpu.make_async_copy(given_ref, inverse_ref, sem)]
        gets[0].start()
        for x_step, part in enumerate(parts):
            x = lax.rem(me_ref[0] + (xs - x_step), xs)
            get = pltpu.make_async_copy(part, weight_ref.at[:, :, x], sems.at[x_step])
            get.start()
            gets.append(get)
        d_gain_ref[...] = jnp.zeros(d_gain_ref.shape, jnp.float32)
        for get in gets:
            get.wait()

    devices, rows, features = value_ref.shape
    d_normed = jnp.dot(
        value_ref[...].reshape(devices * rows, features),
        weight_ref[...].reshape(features, -1),
        preferred_element_type=jnp.float32,
    )
    d_gain = d_gain_ref[...]
    for at in range(devices):
        tokens = slice(at * rows, (at + 1) * rows)
        inverse = column(inverse_ref[pl.ds(step * devices + at, 1), :])
        normed = d_normed[tokens, :]
        scaled = input_ref[tokens, :].astype(jnp.float32) * inverse
        weighted = normed * gain_ref[...]
        d_gain += jnp.sum(normed * scaled, axis=0, keepdims=True)
        inner = jnp.sum(weighted * scaled, axis=1, keepdims=True)
        inner = jnp.transpose(jnp.broadcast_to(inner, (rows, 8)))[0:1, :]
        for peer in range(inner_ref.shape[0]):
            inner_ref[peer, pl.ds(step * devices + at, 1), :] = inner
        base_ref[tokens, :] = grad_ref[tokens, :].astype(jnp.float32) + weighted * inverse
    d_gain_ref[...] = d_gain


def dispatch_kernel(
    width, inverse_ref, inner_ref, slot_ref, gate_ref, given_ref, input_ref, out_ref,
    base_ref, stream_ref, rows_ref, sems, get_sems,
):
    group = input_ref.shape[0]
    experts, capacity, _ = out_ref.shape
    quarter = group // 4
    gets = []
    for at in range(4):
        rows = pl.ds(at * quarter, quarter)
        get = pltpu.make_async_copy(given_ref.at[rows, :], base_ref.at[rows, :], get_sems.at[at])
        get.start()
        gets.append(get)
    inverse = inverse_ref[...]
    inner = jnp.sum(inner_ref[...], axis=0) / width
    factor = jnp.transpose(inner * inverse * inverse)
    tile = group // 8
    for at in range(8):
        rows = slice(at * tile, (at + 1) * tile)
        if at % 2 == 0:
            gets[at // 2].wait()
        stream = (
            base_ref[rows, :]
            - input_ref[rows, :].astype(jnp.float32) * factor[:, at : at + 1]
        )
        stream_ref[rows, :] = stream.astype(jnp.bfloat16)

    puts = []
    for expert in range(experts):
        slot = slot_ref[expert : expert + 1, :]
        gate = gate_ref[expert : expert + 1, :]
        taken = lax.broadcasted_iota(jnp.int32, (capacity, group), 0) == slot
        gates = jnp.sum(jnp.where(taken, gate, 0.0), axis=1, keepdims=True)
        picked = jnp.dot(
            jnp.where(taken, 1.0, 0.0).astype(jnp.bfloat16),
            stream_ref[...],
            preferred_element_type=jnp.float32,
        )
        rows_ref[expert] = (gates * picked).astype(jnp.bfloat16)
        put = pltpu.make_async_copy(rows_ref.at[expert], out_ref.at[expert], sems.at[expert])
        put.start()
        puts.append(put)
    for put in puts:
        put.wait()


def low_split_kernel(me_ref, given_ref, d_gain_ref, *refs):
    outs, (d_value_ref, sem) = refs[:-2], refs[-2:]
    get = pltpu.make_async_copy(given_ref, d_value_ref, sem)
    get.start()
    get.wait()
    count = len(outs)
    rows = d_value_ref.shape[0] // count
    behind = pieces(d_gain_ref[...])
    for k, out in enumerate(outs):
        start = pl.multiple_of(lax.rem(me_ref[0] + k, count) * rows, rows)
        out[0:rows, :] = d_value_ref[pl.ds(start, rows), :].astype(jnp.bfloat16)
        out[rows:, :] = behind


def high_split_kernel(a_ref, b_ref, c_ref, d_ref, out_ref):
    total = a_ref[...].astype(jnp.float32)
    for ref in (b_ref, c_ref, d_ref):
        total += ref[...].astype(jnp.float32)
    count, own, _ = out_ref.shape
    columns = total.shape[1]
    rows = total.shape[0] - PAD
    gain = jnp.sum(total[rows:, :], axis=0, keepdims=True)
    parts = pieces(gain).astype(jnp.float32)
    blocks = columns // 128
    at = lax.broadcasted_iota(jnp.int32, (own, 128), 0)
    behind = jnp.zeros((own, 128), jnp.float32)
    for part in range(3):
        for block in range(blocks):
            row = parts[part : part + 1, block * 128 : (block + 1) * 128]
            behind = jnp.where(at == part * blocks + block, row, behind)
    for to in range(count):
        out_ref[to, :, 0:columns] = total[to * own : (to + 1) * own, :].astype(jnp.bfloat16)
        out_ref[to, :, columns:] = behind.astype(jnp.bfloat16)


def finish_kernel(rescale, parts_ref, d_value_ref, d_gain_ref):
    total = parts_ref[0].astype(jnp.float32)
    for at in range(1, parts_ref.shape[0]):
        total += parts_ref[at].astype(jnp.float32)
    columns = d_value_ref.shape[1]
    d_value_ref[...] = (total[:, 0:columns] * rescale).astype(jnp.bfloat16)
    blocks = columns // 128
    for block in range(blocks):
        gain = total[block : block + 1, columns:]
        for part in (1, 2):
            row = part * blocks + block
            gain += total[row : row + 1, columns:]
        d_gain_ref[:, block * 128 : (block + 1) * 128] = gain * rescale


def to_all(part, axis):
    size = lax.axis_size(axis)
    return lax.all_to_all(
        jnp.broadcast_to(part[None], (size,) + part.shape), axis, 0, 0, tiled=True
    )


def further(part, axis, step):
    size = lax.axis_size(axis)
    return lax.ppermute(part, axis, [(i, (i + step) % size) for i in range(size)])


def on_device(stream_grad, value_grad, attn_input, norm_gain, value_weight, gate_logits, routes):
    group, columns = attn_input.shape
    experts = lax.axis_size(EXPERT)
    zh, zl, xs = lax.axis_size("zh"), lax.axis_size("zl"), lax.axis_size("x")
    width = columns * experts
    tokens_all = group * zh * zl * xs
    rescale = float(tokens_all) ** (-0.5)
    capacity = min(group, 5 * group // (2 * experts))
    rows = value_weight.shape[0]
    features = rows * zh * zl * xs
    own_rows = value_grad.shape[0]
    f32, bf16 = jnp.float32, jnp.bfloat16
    gain_row = norm_gain[None]

    gathered = lax.all_gather(value_grad, EXPERT, axis=0)

    weight = jnp.broadcast_to(value_weight[None], (zh * zl, rows, columns))
    weight = lax.all_to_all(weight, ("zh", "zl"), 0, 0, tiled=True)
    weight = weight.reshape(zh, zl, rows, columns)
    (squares,) = call(squares_kernel, attn_input, out=[((8, group // 8), f32)], limit=24)
    squares = lax.psum(squares, EXPERT)
    normed, inverse = call(
        lambda *refs: norm_kernel(width, *refs), squares, attn_input, gain_row,
        out=[((group, columns), bf16), ((8, group // 8), f32)],
        limit=24,
    )
    weight, normed = lax.optimization_barrier((weight, normed))
    weights = [weight] + [further(weight, "x", step) for step in range(1, xs)]
    gathered, weights[1] = lax.optimization_barrier((gathered, weights[1]))

    slot, gate = call(
        route_kernel, routes.T, gate_logits.T,
        out=[((experts, group), jnp.int32), ((experts, group), f32)],
        limit=24,
    )

    (d_value,) = call(
        value_kernel, gathered, normed,
        out=[((xs, zl, zh, rows, columns), f32)],
        in_specs=[ANY, whole((group, columns))],
        out_specs=[ANY],
        scratch=[
            pltpu.VMEM((experts, own_rows, features), bf16),
            pltpu.VMEM((zh, xs, zl, rows, columns), f32),
            pltpu.SemaphoreType.DMA(()),
            pltpu.SemaphoreType.DMA((zh,)),
        ],
        limit=VALUE_LIMIT,
    )
    d_value = lax.psum_scatter(
        d_value.reshape(features, columns), "x", scatter_dimension=0, tiled=True
    )

    half = pl.BlockSpec((group // 2, columns), lambda i: (i, 0))
    base, inner, own_gain = call(
        normed_kernel, lax.axis_index("x").reshape(1), gathered, attn_input, stream_grad,
        gain_row, inverse, *weights,
        out=[((group, columns), f32), ((experts, 8, group // 8), f32), ((1, columns), f32)],
        in_specs=[
            SMEM,
            pl.BlockSpec((experts // 2, own_rows, features), lambda i: (i, 0, 0)),
            half,
            half,
            whole((1, columns)),
            HBM,
        ]
        + [ANY] * xs,
        out_specs=[half, whole((experts, 8, group // 8)), whole((1, columns))],
        scratch=[
            pltpu.VMEM((8, group // 8), f32),
            pltpu.VMEM((zh, zl, xs, rows, columns), bf16),
            pltpu.SemaphoreType.DMA((xs,)),
            pltpu.SemaphoreType.DMA(()),
        ],
        grid=2,
        limit=NORMED_LIMIT,
        flops=NORMED_FLOPS,
    )
    inner = lax.all_to_all(inner, EXPERT, 0, 0, tiled=True)

    (sent,) = call(
        lambda *refs: dispatch_kernel(width, *refs),
        inverse, inner, slot, gate, base, attn_input,
        out=[((experts, capacity, columns), bf16)],
        in_specs=[
            whole((8, group // 8)),
            whole((experts, 8, group // 8)),
            whole((experts, group)),
            whole((experts, group)),
            ANY,
            whole((group, columns)),
        ],
        out_specs=[ANY],
        scratch=[
            pltpu.VMEM((group, columns), f32),
            pltpu.VMEM((group, columns), bf16),
            pltpu.VMEM((experts, capacity, columns), bf16),
            pltpu.SemaphoreType.DMA((experts,)),
            pltpu.SemaphoreType.DMA((4,)),
        ],
        limit=DISPATCH_LIMIT,
        flops=DISPATCH_FLOPS,
    )
    sent, own_gain = lax.optimization_barrier((sent, own_gain))
    arrived = lax.all_to_all(sent, EXPERT, split_axis=0, concat_axis=2, tiled=True)

    d_gain = lax.psum(own_gain, "x")
    part = (features // xs // zl + PAD, columns)
    parts = call(
        low_split_kernel, lax.axis_index("zl").reshape(1), d_value, d_gain,
        out=[(part, bf16)] * zl, limit=8,
        in_specs=[SMEM, HBM, whole((1, columns))],
        scratch=[pltpu.VMEM((features // xs, columns), f32), pltpu.SemaphoreType.DMA(())],
    )
    parts = [parts[0]] + [further(parts[k], "zl", k) for k in range(1, zl)]
    (parts,) = call(
        high_split_kernel, *parts, out=[((zh, rows, columns + 128), bf16)], limit=8,
    )
    parts = lax.all_to_all(parts, "zh", 0, 0, tiled=True)
    d_value, d_gain = call(
        lambda *refs: finish_kernel(rescale, *refs), parts,
        out=[((rows, columns), bf16), ((1, columns), f32)], limit=8,
    )
    return (d_value, d_gain.reshape(columns), arrived)


def solution(mesh):
    split = Mesh(mesh.devices.reshape(4, 4, 4, 4, 2), ("zh", "zl", "x", "y", "core"))
    dp = ("zh", "zl", "x")
    return jax.shard_map(
        on_device,
        mesh=split,
        in_specs=(
            P(dp, EXPERT),
            P(dp + EXPERT, None),
            P(dp, EXPERT),
            P(EXPERT),
            P(dp, EXPERT),
            P(dp, None),
            P(dp, None),
        ),
        out_specs=(P(dp, EXPERT), P(EXPERT), P(EXPERT, dp, None)),
        check_vma=False,
    )
```

```python
import jax
import jax.numpy as jnp
from jax import lax
from jax.experimental import pallas as pl
from jax.experimental.pallas import tpu as pltpu
from jax.sharding import Mesh, PartitionSpec as P

epsilon = 1e-05
EXPERT = ("y", "core")
ANY = pl.BlockSpec(memory_space=pl.ANY)
HBM = pl.BlockSpec(memory_space=pltpu.HBM)
SMEM = pl.BlockSpec(memory_space=pltpu.SMEM)
PAD = 16
VALUE_LIMIT = 62
NORMED_LIMIT = 52
DISPATCH_LIMIT = 52
NORMED_FLOPS = 4 * 10**9
DISPATCH_FLOPS = 20 * 10**9


def whole(shape):
    return pl.BlockSpec(shape, lambda *at: (0,) * len(shape))


def call(
    kernel, *operands, out, limit=60, grid=1, scratch=(), in_specs=None, out_specs=None, flops=None
):
    cost = {}
    if flops:
        cost["cost_estimate"] = pl.CostEstimate(
            flops=flops, bytes_accessed=10**7, transcendentals=0
        )
    return pl.pallas_call(
        kernel,
        grid=(grid,),
        in_specs=in_specs or [SMEM if o.shape == (1,) else whole(o.shape) for o in operands],
        out_specs=out_specs or [whole(shape) for shape, _ in out],
        out_shape=[jax.ShapeDtypeStruct(shape, kind) for shape, kind in out],
        scratch_shapes=scratch,
        compiler_params=pltpu.CompilerParams(
            dimension_semantics=("arbitrary",), vmem_limit_bytes=limit * 2**20
        ),
        **cost,
    )(*operands)


def column(row):
    return jnp.transpose(jnp.broadcast_to(row, (8, row.shape[1])))[:, 0:1]


def pieces(row):
    high = row.astype(jnp.bfloat16).astype(jnp.float32)
    middle = (row - high).astype(jnp.bfloat16).astype(jnp.float32)
    low = row - high - middle
    at = lax.broadcasted_iota(jnp.int32, (PAD, row.shape[1]), 0)
    rows = jnp.where(at == 0, high, jnp.where(at == 1, middle, jnp.where(at == 2, low, 0.0)))
    return rows.astype(jnp.bfloat16)


def pack_kernel(value_ref, input_ref, weight_ref, packed_ref, copies_ref):
    rows = value_ref.shape[0]
    inputs = input_ref[...].astype(jnp.float32)
    squares = jnp.sum(inputs * inputs, axis=1, keepdims=True)
    row = jnp.transpose(jnp.broadcast_to(squares, (squares.shape[0], 8)))[0:1, :]
    packed_ref[0:rows, :] = value_ref[...]
    packed_ref[rows:, :] = pieces(row)
    for peer in range(copies_ref.shape[0]):
        copies_ref[peer] = weight_ref[...]


def route_kernel(routes_ref, logits_ref, slot_ref, gate_ref):
    experts, group = slot_ref.shape
    expert = lax.broadcasted_iota(jnp.int32, (experts, group), 0)
    first = routes_ref[0:1, :] == expert
    second = routes_ref[1:2, :] == expert
    named = jnp.where(first | second, 1.0, 0.0)
    earlier = lax.broadcasted_iota(jnp.int32, (group, group), 0) < lax.broadcasted_iota(
        jnp.int32, (group, group), 1
    )
    count = jnp.dot(
        named.astype(jnp.bfloat16),
        jnp.where(earlier, 1.0, 0.0).astype(jnp.bfloat16),
        preferred_element_type=jnp.float32,
    )
    slot_ref[...] = jnp.where(named > 0.0, count, -1.0).astype(jnp.int32)
    low, high = logits_ref[0:1, :], logits_ref[1:2, :]
    gate_first = 1.0 / (1.0 + jnp.exp(high - low))
    gate_second = 1.0 / (1.0 + jnp.exp(low - high))
    gate_ref[...] = jnp.where(first, gate_first, jnp.where(second, gate_second, 0.0))


def value_kernel(
    width, gathered_ref, whole_input_ref, gain_ref, d_value_ref, inverse_ref,
    squares_ref, input_ref, value_ref, normed_ref, partial_ref, sems,
):
    devices, rows, features = value_ref.shape
    group = input_ref.shape[0]
    get_squares = pltpu.make_async_copy(
        gathered_ref.at[:, pl.ds(rows, PAD), :], squares_ref, sems.at[0]
    )
    get_value = pltpu.make_async_copy(
        gathered_ref.at[:, pl.ds(0, rows), :], value_ref, sems.at[1]
    )
    get_input = pltpu.make_async_copy(whole_input_ref, input_ref, sems.at[2])
    get_squares.start()
    get_input.start()
    get_value.start()
    get_squares.wait()
    squares = jnp.zeros((1, group), jnp.float32)
    for device in range(devices):
        part = squares_ref[device].astype(jnp.float32)
        squares += jnp.sum(part, axis=0, keepdims=True)
    inverse = 1.0 / jnp.sqrt(squares / width + epsilon)
    tile = group // 8
    for at in range(8):
        inverse_ref[at : at + 1, :] = inverse[:, at * tile : (at + 1) * tile]
    get_input.wait()
    scaled = input_ref[...].astype(jnp.float32) * column(inverse)
    normed_ref[...] = (scaled * gain_ref[...]).astype(jnp.bfloat16)

    zh, xs, zl, own, _ = partial_ref.shape
    block = features // zh
    get_value.wait()
    puts = []
    for high in range(zh):
        partial = lax.dot_general(
            value_ref[:, :, high * block : (high + 1) * block].reshape(group, block),
            normed_ref[...],
            (((0,), (0,)), ((), ())),
            preferred_element_type=jnp.float32,
        )
        for low in range(zl):
            for x in range(xs):
                start = (low * xs + x) * own
                partial_ref[high, x, low] = partial[start : start + own, :]
        put = pltpu.make_async_copy(
            partial_ref.at[high], d_value_ref.at[:, :, high], sems.at[3 + high]
        )
        put.start()
        puts.append(put)
    for put in puts:
        put.wait()


def normed_kernel(
    me_ref, value_ref, input_ref, grad_ref, gain_ref, given_ref, *refs
):
    parts = refs[:-7]
    base_ref, inner_ref, d_gain_ref, inverse_ref, weight_ref, sems, sem = refs[-7:]
    step = pl.program_id(0)

    @pl.when(step == 0)
    def _():
        xs = len(parts)
        gets = [pltpu.make_async_copy(given_ref, inverse_ref, sem)]
        gets[0].start()
        for x_step, part in enumerate(parts):
            x = lax.rem(me_ref[0] + (xs - x_step), xs)
            get = pltpu.make_async_copy(part, weight_ref.at[:, :, x], sems.at[x_step])
            get.start()
            gets.append(get)
        d_gain_ref[...] = jnp.zeros(d_gain_ref.shape, jnp.float32)
        for get in gets:
            get.wait()

    devices, rows, features = value_ref.shape
    d_normed = jnp.dot(
        value_ref[...].reshape(devices * rows, features),
        weight_ref[...].reshape(features, -1),
        preferred_element_type=jnp.float32,
    )
    d_gain = d_gain_ref[...]
    for at in range(devices):
        tokens = slice(at * rows, (at + 1) * rows)
        inverse = column(inverse_ref[pl.ds(step * devices + at, 1), :])
        normed = d_normed[tokens, :]
        scaled = input_ref[tokens, :].astype(jnp.float32) * inverse
        weighted = normed * gain_ref[...]
        d_gain += jnp.sum(normed * scaled, axis=0, keepdims=True)
        inner = jnp.sum(weighted * scaled, axis=1, keepdims=True)
        inner = jnp.transpose(jnp.broadcast_to(inner, (rows, 8)))[0:1, :]
        for peer in range(inner_ref.shape[0]):
            inner_ref[peer, pl.ds(step * devices + at, 1), :] = inner
        base_ref[tokens, :] = grad_ref[tokens, :].astype(jnp.float32) + weighted * inverse
    d_gain_ref[...] = d_gain


def dispatch_kernel(
    width, inverse_ref, inner_ref, slot_ref, gate_ref, given_ref, input_ref, out_ref,
    base_ref, stream_ref, rows_ref, sems, get_sems,
):
    group = input_ref.shape[0]
    experts, capacity, _ = out_ref.shape
    quarter = group // 4
    gets = []
    for at in range(4):
        rows = pl.ds(at * quarter, quarter)
        get = pltpu.make_async_copy(given_ref.at[rows, :], base_ref.at[rows, :], get_sems.at[at])
        get.start()
        gets.append(get)
    inverse = inverse_ref[...]
    inner = jnp.sum(inner_ref[...], axis=0) / width
    factor = jnp.transpose(inner * inverse * inverse)
    tile = group // 8
    for at in range(8):
        rows = slice(at * tile, (at + 1) * tile)
        if at % 2 == 0:
            gets[at // 2].wait()
        stream = (
            base_ref[rows, :]
            - input_ref[rows, :].astype(jnp.float32) * factor[:, at : at + 1]
        )
        stream_ref[rows, :] = stream.astype(jnp.bfloat16)

    puts = []
    for expert in range(experts):
        slot = slot_ref[expert : expert + 1, :]
        gate = gate_ref[expert : expert + 1, :]
        taken = lax.broadcasted_iota(jnp.int32, (capacity, group), 0) == slot
        gates = jnp.sum(jnp.where(taken, gate, 0.0), axis=1, keepdims=True)
        picked = jnp.dot(
            jnp.where(taken, 1.0, 0.0).astype(jnp.bfloat16),
            stream_ref[...],
            preferred_element_type=jnp.float32,
        )
        rows_ref[expert] = (gates * picked).astype(jnp.bfloat16)
        put = pltpu.make_async_copy(rows_ref.at[expert], out_ref.at[expert], sems.at[expert])
        put.start()
        puts.append(put)
    for put in puts:
        put.wait()


def low_split_kernel(me_ref, given_ref, d_gain_ref, *refs):
    outs, (d_value_ref, sem) = refs[:-2], refs[-2:]
    get = pltpu.make_async_copy(given_ref, d_value_ref, sem)
    get.start()
    get.wait()
    count = len(outs)
    rows = d_value_ref.shape[0] // count
    behind = pieces(d_gain_ref[...])
    for k, out in enumerate(outs):
        start = pl.multiple_of(lax.rem(me_ref[0] + k, count) * rows, rows)
        out[0:rows, :] = d_value_ref[pl.ds(start, rows), :].astype(jnp.bfloat16)
        out[rows:, :] = behind


def high_split_kernel(me_ref, a_ref, b_ref, c_ref, d_ref, *refs):
    outs, total_ref = refs[:-1], refs[-1]
    total = a_ref[...].astype(jnp.float32)
    for ref in (b_ref, c_ref, d_ref):
        total += ref[...].astype(jnp.float32)
    count, own = len(outs), outs[0].shape[0]
    columns = total.shape[1]
    rows = total.shape[0] - PAD
    total_ref[...] = total
    gain = jnp.sum(total[rows:, :], axis=0, keepdims=True)
    parts = pieces(gain).astype(jnp.float32)
    blocks = columns // 128
    at = lax.broadcasted_iota(jnp.int32, (own, 128), 0)
    behind = jnp.zeros((own, 128), jnp.float32)
    for part in range(3):
        for block in range(blocks):
            row = parts[part : part + 1, block * 128 : (block + 1) * 128]
            behind = jnp.where(at == part * blocks + block, row, behind)
    for k, out in enumerate(outs):
        start = pl.multiple_of(lax.rem(me_ref[0] + k, count) * own, own)
        out[:, 0:columns] = total_ref[pl.ds(start, own), :].astype(jnp.bfloat16)
        out[:, columns:] = behind.astype(jnp.bfloat16)


def finish_kernel(rescale, a_ref, b_ref, c_ref, d_ref, d_value_ref, d_gain_ref):
    total = a_ref[...].astype(jnp.float32)
    for ref in (b_ref, c_ref, d_ref):
        total += ref[...].astype(jnp.float32)
    columns = d_value_ref.shape[1]
    d_value_ref[...] = (total[:, 0:columns] * rescale).astype(jnp.bfloat16)
    blocks = columns // 128
    for block in range(blocks):
        gain = total[block : block + 1, columns:]
        for part in (1, 2):
            row = part * blocks + block
            gain += total[row : row + 1, columns:]
        d_gain_ref[:, block * 128 : (block + 1) * 128] = gain * rescale


def to_all(part, axis):
    size = lax.axis_size(axis)
    return lax.all_to_all(
        jnp.broadcast_to(part[None], (size,) + part.shape), axis, 0, 0, tiled=True
    )


def further(part, axis, step):
    size = lax.axis_size(axis)
    return lax.ppermute(part, axis, [(i, (i + step) % size) for i in range(size)])


def on_device(stream_grad, value_grad, attn_input, norm_gain, value_weight, gate_logits, routes):
    group, columns = attn_input.shape
    experts = lax.axis_size(EXPERT)
    zh, zl, xs = lax.axis_size("zh"), lax.axis_size("zl"), lax.axis_size("x")
    width = columns * experts
    tokens_all = group * zh * zl * xs
    rescale = float(tokens_all) ** (-0.5)
    capacity = min(group, 5 * group // (2 * experts))
    rows = value_weight.shape[0]
    features = rows * zh * zl * xs
    own_rows = value_grad.shape[0]
    f32, bf16 = jnp.float32, jnp.bfloat16
    gain_row = norm_gain[None]

    packed, copies = call(
        pack_kernel, value_grad, attn_input, value_weight,
        out=[((own_rows + PAD, features), bf16), ((zh * zl, rows, columns), bf16)],
    )
    gathered = lax.all_gather(packed, EXPERT, axis=0)

    weight = lax.all_to_all(copies, ("zh", "zl"), 0, 0, tiled=True)
    weight = weight.reshape(zh, zl, rows, columns)
    weights = [weight] + [further(weight, "x", step) for step in range(1, xs)]
    gathered, weights[1] = lax.optimization_barrier((gathered, weights[1]))

    slot, gate = call(
        route_kernel, routes.T, gate_logits.T,
        out=[((experts, group), jnp.int32), ((experts, group), f32)],
        limit=24,
    )

    d_value, inverse = call(
        lambda *refs: value_kernel(width, *refs), gathered, attn_input, gain_row,
        out=[((xs, zl, zh, rows, columns), f32), ((8, group // 8), f32)],
        in_specs=[ANY, ANY, whole((1, columns))],
        out_specs=[ANY, whole((8, group // 8))],
        scratch=[
            pltpu.VMEM((experts, PAD, features), bf16),
            pltpu.VMEM((group, columns), bf16),
            pltpu.VMEM((experts, own_rows, features), bf16),
            pltpu.VMEM((group, columns), bf16),
            pltpu.VMEM((zh, xs, zl, rows, columns), f32),
            pltpu.SemaphoreType.DMA((3 + zh,)),
        ],
        limit=VALUE_LIMIT,
    )
    d_value = lax.psum_scatter(
        d_value.reshape(features, columns), "x", scatter_dimension=0, tiled=True
    )

    half = pl.BlockSpec((group // 2, columns), lambda i: (i, 0))
    base, inner, own_gain = call(
        normed_kernel, lax.axis_index("x").reshape(1), gathered, attn_input, stream_grad,
        gain_row, inverse, *weights,
        out=[((group, columns), f32), ((experts, 8, group // 8), f32), ((1, columns), f32)],
        in_specs=[
            SMEM,
            pl.BlockSpec((experts // 2, own_rows, features), lambda i: (i, 0, 0)),
            half,
            half,
            whole((1, columns)),
            HBM,
        ]
        + [ANY] * xs,
        out_specs=[half, whole((experts, 8, group // 8)), whole((1, columns))],
        scratch=[
            pltpu.VMEM((8, group // 8), f32),
            pltpu.VMEM((zh, zl, xs, rows, columns), bf16),
            pltpu.SemaphoreType.DMA((xs,)),
            pltpu.SemaphoreType.DMA(()),
        ],
        grid=2,
        limit=NORMED_LIMIT,
        flops=NORMED_FLOPS,
    )
    inner = lax.all_to_all(inner, EXPERT, 0, 0, tiled=True)

    (sent,) = call(
        lambda *refs: dispatch_kernel(width, *refs),
        inverse, inner, slot, gate, base, attn_input,
        out=[((experts, capacity, columns), bf16)],
        in_specs=[
            whole((8, group // 8)),
            whole((experts, 8, group // 8)),
            whole((experts, group)),
            whole((experts, group)),
            ANY,
            whole((group, columns)),
        ],
        out_specs=[ANY],
        scratch=[
            pltpu.VMEM((group, columns), f32),
            pltpu.VMEM((group, columns), bf16),
            pltpu.VMEM((experts, capacity, columns), bf16),
            pltpu.SemaphoreType.DMA((experts,)),
            pltpu.SemaphoreType.DMA((4,)),
        ],
        limit=DISPATCH_LIMIT,
        flops=DISPATCH_FLOPS,
    )
    sent, own_gain = lax.optimization_barrier((sent, own_gain))
    arrived = lax.all_to_all(sent, EXPERT, split_axis=0, concat_axis=2, tiled=True)

    d_gain = lax.psum(own_gain, "x")
    part = (features // xs // zl + PAD, columns)
    parts = call(
        low_split_kernel, lax.axis_index("zl").reshape(1), d_value, d_gain,
        out=[(part, bf16)] * zl, limit=8,
        in_specs=[SMEM, HBM, whole((1, columns))],
        scratch=[pltpu.VMEM((features // xs, columns), f32), pltpu.SemaphoreType.DMA(())],
    )
    parts = [parts[0]] + [further(parts[k], "zl", k) for k in range(1, zl)]
    parts = call(
        high_split_kernel, lax.axis_index("zh").reshape(1), *parts,
        out=[((rows, columns + 128), bf16)] * zh, limit=8,
        scratch=[pltpu.VMEM(parts[0].shape, f32)],
    )
    parts = [parts[0]] + [further(parts[k], "zh", k) for k in range(1, zh)]
    d_value, d_gain = call(
        lambda *refs: finish_kernel(rescale, *refs), *parts,
        out=[((rows, columns), bf16), ((1, columns), f32)], limit=8,
    )
    return (d_value, d_gain.reshape(columns), arrived)


def solution(mesh):
    split = Mesh(mesh.devices.reshape(4, 4, 4, 4, 2), ("zh", "zl", "x", "y", "core"))
    dp = ("zh", "zl", "x")
    return jax.shard_map(
        on_device,
        mesh=split,
        in_specs=(
            P(dp, EXPERT),
            P(dp + EXPERT, None),
            P(dp, EXPERT),
            P(EXPERT),
            P(dp, EXPERT),
            P(dp, None),
            P(dp, None),
        ),
        out_specs=(P(dp, EXPERT), P(EXPERT), P(EXPERT, dp, None)),
        check_vma=False,
    )
```

```python
import jax
import jax.numpy as jnp
from jax import lax
from jax.experimental import pallas as pl
from jax.experimental.pallas import tpu as pltpu
from jax.sharding import Mesh, PartitionSpec as P

epsilon = 1e-05
EXPERT = ("y", "core")
ANY = pl.BlockSpec(memory_space=pl.ANY)
HBM = pl.BlockSpec(memory_space=pltpu.HBM)
SMEM = pl.BlockSpec(memory_space=pltpu.SMEM)
PAD = 16
VALUE_LIMIT = 62
NORMED_LIMIT = 52
DISPATCH_LIMIT = 57
NORMED_FLOPS = 4 * 10**9
DISPATCH_FLOPS = 20 * 10**9


def whole(shape):
    return pl.BlockSpec(shape, lambda *at: (0,) * len(shape))


def call(
    kernel, *operands, out, limit=60, grid=1, scratch=(), in_specs=None, out_specs=None, flops=None
):
    cost = {}
    if flops:
        cost["cost_estimate"] = pl.CostEstimate(
            flops=flops, bytes_accessed=10**7, transcendentals=0
        )
    return pl.pallas_call(
        kernel,
        grid=(grid,),
        in_specs=in_specs or [SMEM if o.shape == (1,) else whole(o.shape) for o in operands],
        out_specs=out_specs or [whole(shape) for shape, _ in out],
        out_shape=[jax.ShapeDtypeStruct(shape, kind) for shape, kind in out],
        scratch_shapes=scratch,
        compiler_params=pltpu.CompilerParams(
            dimension_semantics=("arbitrary",), vmem_limit_bytes=limit * 2**20
        ),
        **cost,
    )(*operands)


def column(row):
    return jnp.transpose(jnp.broadcast_to(row, (8, row.shape[1])))[:, 0:1]


def pieces(row):
    high = row.astype(jnp.bfloat16).astype(jnp.float32)
    middle = (row - high).astype(jnp.bfloat16).astype(jnp.float32)
    low = row - high - middle
    at = lax.broadcasted_iota(jnp.int32, (PAD, row.shape[1]), 0)
    rows = jnp.where(at == 0, high, jnp.where(at == 1, middle, jnp.where(at == 2, low, 0.0)))
    return rows.astype(jnp.bfloat16)


def pack_kernel(value_ref, input_ref, weight_ref, packed_ref, copies_ref):
    rows = value_ref.shape[0]
    inputs = input_ref[...].astype(jnp.float32)
    squares = jnp.sum(inputs * inputs, axis=1, keepdims=True)
    row = jnp.transpose(jnp.broadcast_to(squares, (squares.shape[0], 8)))[0:1, :]
    packed_ref[0:rows, :] = value_ref[...]
    packed_ref[rows:, :] = pieces(row)
    for peer in range(copies_ref.shape[0]):
        copies_ref[peer] = weight_ref[...]


def route_kernel(routes_ref, logits_ref, slot_ref, gate_ref):
    experts, group = slot_ref.shape
    expert = lax.broadcasted_iota(jnp.int32, (experts, group), 0)
    first = routes_ref[0:1, :] == expert
    second = routes_ref[1:2, :] == expert
    named = jnp.where(first | second, 1.0, 0.0)
    earlier = lax.broadcasted_iota(jnp.int32, (group, group), 0) < lax.broadcasted_iota(
        jnp.int32, (group, group), 1
    )
    count = jnp.dot(
        named.astype(jnp.bfloat16),
        jnp.where(earlier, 1.0, 0.0).astype(jnp.bfloat16),
        preferred_element_type=jnp.float32,
    )
    slot_ref[...] = jnp.where(named > 0.0, count, -1.0).astype(jnp.int32)
    low, high = logits_ref[0:1, :], logits_ref[1:2, :]
    gate_first = 1.0 / (1.0 + jnp.exp(high - low))
    gate_second = 1.0 / (1.0 + jnp.exp(low - high))
    gate_ref[...] = jnp.where(first, gate_first, jnp.where(second, gate_second, 0.0))


def value_kernel(
    width, gathered_ref, whole_input_ref, gain_ref, d_value_ref, inverse_ref,
    squares_ref, input_ref, value_ref, normed_ref, partial_ref, sems,
):
    devices, rows, features = value_ref.shape
    group = input_ref.shape[0]
    get_squares = pltpu.make_async_copy(
        gathered_ref.at[:, pl.ds(rows, PAD), :], squares_ref, sems.at[0]
    )
    get_value = pltpu.make_async_copy(
        gathered_ref.at[:, pl.ds(0, rows), :], value_ref, sems.at[1]
    )
    get_input = pltpu.make_async_copy(whole_input_ref, input_ref, sems.at[2])
    get_squares.start()
    get_input.start()
    get_value.start()
    get_squares.wait()
    squares = jnp.zeros((1, group), jnp.float32)
    for device in range(devices):
        part = squares_ref[device].astype(jnp.float32)
        squares += jnp.sum(part, axis=0, keepdims=True)
    inverse = 1.0 / jnp.sqrt(squares / width + epsilon)
    tile = group // 8
    for at in range(8):
        inverse_ref[at : at + 1, :] = inverse[:, at * tile : (at + 1) * tile]
    get_input.wait()
    scaled = input_ref[...].astype(jnp.float32) * column(inverse)
    normed_ref[...] = (scaled * gain_ref[...]).astype(jnp.bfloat16)

    zh, xs, zl, own, _ = partial_ref.shape
    block = features // zh
    get_value.wait()
    puts = []
    for high in range(zh):
        partial = lax.dot_general(
            value_ref[:, :, high * block : (high + 1) * block].reshape(group, block),
            normed_ref[...],
            (((0,), (0,)), ((), ())),
            preferred_element_type=jnp.float32,
        )
        for low in range(zl):
            for x in range(xs):
                start = (low * xs + x) * own
                partial_ref[high, x, low] = partial[start : start + own, :]
        put = pltpu.make_async_copy(
            partial_ref.at[high], d_value_ref.at[:, :, high], sems.at[3 + high]
        )
        put.start()
        puts.append(put)
    for put in puts:
        put.wait()


def normed_kernel(
    me_ref, value_ref, input_ref, grad_ref, gain_ref, given_ref, *refs
):
    parts = refs[:-7]
    base_ref, inner_ref, d_gain_ref, inverse_ref, weight_ref, sems, sem = refs[-7:]
    step = pl.program_id(0)

    @pl.when(step == 0)
    def _():
        xs = len(parts)
        gets = [pltpu.make_async_copy(given_ref, inverse_ref, sem)]
        gets[0].start()
        for x_step, part in enumerate(parts):
            x = lax.rem(me_ref[0] + (xs - x_step), xs)
            get = pltpu.make_async_copy(part, weight_ref.at[:, :, x], sems.at[x_step])
            get.start()
            gets.append(get)
        d_gain_ref[...] = jnp.zeros(d_gain_ref.shape, jnp.float32)
        for get in gets:
            get.wait()

    devices, rows, features = value_ref.shape
    d_normed = jnp.dot(
        value_ref[...].reshape(devices * rows, features),
        weight_ref[...].reshape(features, -1),
        preferred_element_type=jnp.float32,
    )
    d_gain = d_gain_ref[...]
    for at in range(devices):
        tokens = slice(at * rows, (at + 1) * rows)
        inverse = column(inverse_ref[pl.ds(step * devices + at, 1), :])
        normed = d_normed[tokens, :]
        scaled = input_ref[tokens, :].astype(jnp.float32) * inverse
        weighted = normed * gain_ref[...]
        d_gain += jnp.sum(normed * scaled, axis=0, keepdims=True)
        inner = jnp.sum(weighted * scaled, axis=1, keepdims=True)
        inner = jnp.transpose(jnp.broadcast_to(inner, (rows, 8)))[0:1, :]
        for peer in range(inner_ref.shape[0]):
            inner_ref[peer, pl.ds(step * devices + at, 1), :] = inner
        base_ref[tokens, :] = grad_ref[tokens, :].astype(jnp.float32) + weighted * inverse
    d_gain_ref[...] = d_gain


def dispatch_kernel(
    width, inverse_ref, inner_ref, slot_ref, gate_ref, given_ref, input_ref, out_ref,
    base_ref, stream_ref, rows_ref, sems, get_sems,
):
    group = input_ref.shape[0]
    experts, capacity, _ = out_ref.shape
    quarter = group // 4
    gets = []
    for at in range(4):
        rows = pl.ds(at * quarter, quarter)
        get = pltpu.make_async_copy(given_ref.at[rows, :], base_ref.at[rows, :], get_sems.at[at])
        get.start()
        gets.append(get)
    inverse = inverse_ref[...]
    inner = jnp.sum(inner_ref[...], axis=0) / width
    factor = jnp.transpose(inner * inverse * inverse)
    tile = group // 8
    for at in range(8):
        rows = slice(at * tile, (at + 1) * tile)
        if at % 2 == 0:
            gets[at // 2].wait()
        stream = (
            base_ref[rows, :]
            - input_ref[rows, :].astype(jnp.float32) * factor[:, at : at + 1]
        )
        stream_ref[rows, :] = stream.astype(jnp.bfloat16)

    puts = []
    for expert in range(experts):
        slot = slot_ref[expert : expert + 1, :]
        gate = gate_ref[expert : expert + 1, :]
        taken = lax.broadcasted_iota(jnp.int32, (capacity, group), 0) == slot
        gates = jnp.sum(jnp.where(taken, gate, 0.0), axis=1, keepdims=True)
        picked = jnp.dot(
            jnp.where(taken, 1.0, 0.0).astype(jnp.bfloat16),
            stream_ref[...],
            preferred_element_type=jnp.float32,
        )
        rows_ref[expert] = (gates * picked).astype(jnp.bfloat16)
        put = pltpu.make_async_copy(rows_ref.at[expert], out_ref.at[expert], sems.at[expert])
        put.start()
        puts.append(put)
    for put in puts:
        put.wait()


def low_split_kernel(me_ref, given_ref, d_gain_ref, *refs):
    outs, (d_value_ref, sem) = refs[:-2], refs[-2:]
    get = pltpu.make_async_copy(given_ref, d_value_ref, sem)
    get.start()
    get.wait()
    count = len(outs)
    rows = d_value_ref.shape[0] // count
    behind = pieces(d_gain_ref[...])
    for k, out in enumerate(outs):
        start = pl.multiple_of(lax.rem(me_ref[0] + k, count) * rows, rows)
        out[0:rows, :] = d_value_ref[pl.ds(start, rows), :].astype(jnp.bfloat16)
        out[rows:, :] = behind


def high_split_kernel(me_ref, a_ref, b_ref, c_ref, d_ref, *refs):
    outs, total_ref = refs[:-1], refs[-1]
    total = a_ref[...].astype(jnp.float32)
    for ref in (b_ref, c_ref, d_ref):
        total += ref[...].astype(jnp.float32)
    count, own = len(outs), outs[0].shape[0]
    columns = total.shape[1]
    rows = total.shape[0] - PAD
    total_ref[...] = total
    gain = jnp.sum(total[rows:, :], axis=0, keepdims=True)
    parts = pieces(gain).astype(jnp.float32)
    blocks = columns // 128
    at = lax.broadcasted_iota(jnp.int32, (own, 128), 0)
    behind = jnp.zeros((own, 128), jnp.float32)
    for part in range(3):
        for block in range(blocks):
            row = parts[part : part + 1, block * 128 : (block + 1) * 128]
            behind = jnp.where(at == part * blocks + block, row, behind)
    for k, out in enumerate(outs):
        start = pl.multiple_of(lax.rem(me_ref[0] + k, count) * own, own)
        out[:, 0:columns] = total_ref[pl.ds(start, own), :].astype(jnp.bfloat16)
        out[:, columns:] = behind.astype(jnp.bfloat16)


def finish_kernel(rescale, a_ref, b_ref, c_ref, d_ref, d_value_ref, d_gain_ref):
    total = a_ref[...].astype(jnp.float32)
    for ref in (b_ref, c_ref, d_ref):
        total += ref[...].astype(jnp.float32)
    columns = d_value_ref.shape[1]
    d_value_ref[...] = (total[:, 0:columns] * rescale).astype(jnp.bfloat16)
    blocks = columns // 128
    for block in range(blocks):
        gain = total[block : block + 1, columns:]
        for part in (1, 2):
            row = part * blocks + block
            gain += total[row : row + 1, columns:]
        d_gain_ref[:, block * 128 : (block + 1) * 128] = gain * rescale


def to_all(part, axis):
    size = lax.axis_size(axis)
    return lax.all_to_all(
        jnp.broadcast_to(part[None], (size,) + part.shape), axis, 0, 0, tiled=True
    )


def further(part, axis, step):
    size = lax.axis_size(axis)
    return lax.ppermute(part, axis, [(i, (i + step) % size) for i in range(size)])


def on_device(stream_grad, value_grad, attn_input, norm_gain, value_weight, gate_logits, routes):
    group, columns = attn_input.shape
    experts = lax.axis_size(EXPERT)
    zh, zl, xs = lax.axis_size("zh"), lax.axis_size("zl"), lax.axis_size("x")
    width = columns * experts
    tokens_all = group * zh * zl * xs
    rescale = float(tokens_all) ** (-0.5)
    capacity = min(group, 5 * group // (2 * experts))
    rows = value_weight.shape[0]
    features = rows * zh * zl * xs
    own_rows = value_grad.shape[0]
    f32, bf16 = jnp.float32, jnp.bfloat16
    gain_row = norm_gain[None]

    packed, copies = call(
        pack_kernel, value_grad, attn_input, value_weight,
        out=[((own_rows + PAD, features), bf16), ((zh * zl, rows, columns), bf16)],
    )
    gathered = lax.all_gather(packed, EXPERT, axis=0)

    weight = lax.all_to_all(copies, ("zh", "zl"), 0, 0, tiled=True)
    weight = weight.reshape(zh, zl, rows, columns)
    weights = [weight] + [further(weight, "x", step) for step in range(1, xs)]
    gathered, weights[1] = lax.optimization_barrier((gathered, weights[1]))

    slot, gate = call(
        route_kernel, routes.T, gate_logits.T,
        out=[((experts, group), jnp.int32), ((experts, group), f32)],
        limit=24,
    )

    d_value, inverse = call(
        lambda *refs: value_kernel(width, *refs), gathered, attn_input, gain_row,
        out=[((xs, zl, zh, rows, columns), f32), ((8, group // 8), f32)],
        in_specs=[ANY, ANY, whole((1, columns))],
        out_specs=[ANY, whole((8, group // 8))],
        scratch=[
            pltpu.VMEM((experts, PAD, features), bf16),
            pltpu.VMEM((group, columns), bf16),
            pltpu.VMEM((experts, own_rows, features), bf16),
            pltpu.VMEM((group, columns), bf16),
            pltpu.VMEM((zh, xs, zl, rows, columns), f32),
            pltpu.SemaphoreType.DMA((3 + zh,)),
        ],
        limit=VALUE_LIMIT,
    )
    d_value = lax.psum_scatter(
        d_value.reshape(features, columns), "x", scatter_dimension=0, tiled=True
    )

    half = pl.BlockSpec((group // 2, columns), lambda i: (i, 0))
    base, inner, own_gain = call(
        normed_kernel, lax.axis_index("x").reshape(1), gathered, attn_input, stream_grad,
        gain_row, inverse, *weights,
        out=[((group, columns), f32), ((experts, 8, group // 8), f32), ((1, columns), f32)],
        in_specs=[
            SMEM,
            pl.BlockSpec((experts // 2, own_rows, features), lambda i: (i, 0, 0)),
            half,
            half,
            whole((1, columns)),
            HBM,
        ]
        + [ANY] * xs,
        out_specs=[half, whole((experts, 8, group // 8)), whole((1, columns))],
        scratch=[
            pltpu.VMEM((8, group // 8), f32),
            pltpu.VMEM((zh, zl, xs, rows, columns), bf16),
            pltpu.SemaphoreType.DMA((xs,)),
            pltpu.SemaphoreType.DMA(()),
        ],
        grid=2,
        limit=NORMED_LIMIT,
        flops=NORMED_FLOPS,
    )
    inner = lax.all_to_all(inner, EXPERT, 0, 0, tiled=True)

    (sent,) = call(
        lambda *refs: dispatch_kernel(width, *refs),
        inverse, inner, slot, gate, base, attn_input,
        out=[((experts, capacity, columns), bf16)],
        in_specs=[
            whole((8, group // 8)),
            whole((experts, 8, group // 8)),
            whole((experts, group)),
            whole((experts, group)),
            ANY,
            whole((group, columns)),
        ],
        out_specs=[ANY],
        scratch=[
            pltpu.VMEM((group, columns), f32),
            pltpu.VMEM((group, columns), bf16),
            pltpu.VMEM((experts, capacity, columns), bf16),
            pltpu.SemaphoreType.DMA((experts,)),
            pltpu.SemaphoreType.DMA((4,)),
        ],
        limit=DISPATCH_LIMIT,
        flops=DISPATCH_FLOPS,
    )
    sent, own_gain = lax.optimization_barrier((sent, own_gain))
    arrived = lax.all_to_all(sent, EXPERT, split_axis=0, concat_axis=2, tiled=True)

    d_gain = lax.psum(own_gain, "x")
    part = (features // xs // zl + PAD, columns)
    parts = call(
        low_split_kernel, lax.axis_index("zl").reshape(1), d_value, d_gain,
        out=[(part, bf16)] * zl, limit=8,
        in_specs=[SMEM, HBM, whole((1, columns))],
        scratch=[pltpu.VMEM((features // xs, columns), f32), pltpu.SemaphoreType.DMA(())],
    )
    parts = [parts[0]] + [further(parts[k], "zl", k) for k in range(1, zl)]
    parts = call(
        high_split_kernel, lax.axis_index("zh").reshape(1), *parts,
        out=[((rows, columns + 128), bf16)] * zh, limit=8,
        scratch=[pltpu.VMEM(parts[0].shape, f32)],
    )
    parts = [parts[0]] + [further(parts[k], "zh", k) for k in range(1, zh)]
    d_value, d_gain = call(
        lambda *refs: finish_kernel(rescale, *refs), *parts,
        out=[((rows, columns), bf16), ((1, columns), f32)], limit=8,
    )
    return (d_value, d_gain.reshape(columns), arrived)


def solution(mesh):
    split = Mesh(mesh.devices.reshape(4, 4, 4, 4, 2), ("zh", "zl", "x", "y", "core"))
    dp = ("zh", "zl", "x")
    return jax.shard_map(
        on_device,
        mesh=split,
        in_specs=(
            P(dp, EXPERT),
            P(dp + EXPERT, None),
            P(dp, EXPERT),
            P(EXPERT),
            P(dp, EXPERT),
            P(dp, None),
            P(dp, None),
        ),
        out_specs=(P(dp, EXPERT), P(EXPERT), P(EXPERT, dp, None)),
        check_vma=False,
    )
```
